128 devices in a mesh: seq: 128 (over x, y, z, core).
Axes of the slice: x: 4, y: 4, z: 4, core: 2. Of those that a mesh axis runs over, the one named last changes fastest.
Arguments:
- parent_rows: bfloat16 [32768, 512], P('seq'), may hold values from -50 to 50, as said below
- counts: int32 [32768], P('seq'), may hold values from 0 to 8, as said below
- occupancy: int32 [65536], P('seq'), may hold values from 1 to 255
- sib_table: bfloat16 [8, 512], replicated, may hold values from -6 to 6
- gain: float32 [512], replicated, may hold values from 0.1 to 1.9
- w_qkv: bfloat16 [512, 1536], replicated, may hold values from -0.25 to 0.25
- w_out: bfloat16 [512, 512], replicated, may hold values from -0.25 to 0.25
- w_head: bfloat16 [512, 8], replicated, may hold values from -0.25 to 0.25
Outputs:
- grad_qkv: float32 [512, 1536], replicated
- grad_out: float32 [512, 512], replicated
- grad_head: float32 [512, 8], replicated
- grad_gain: float32 [512], replicated
- grad_sib: float32 [8, 512], replicated
The draws below stay inside these ranges and needn't reach their ends.
Inputs may be any that keep to these rules, and one draw needn't show every extreme that they name: `parent_rows`: each value is a random draw times a scale of its row and a scale of its column. The counts add up to 65536. The children of the parents held by device k form the contiguous range of nodes given by the counts, and lie on devices k-1, k and k+1. In each device's 256 parents, some parent has 8 children and some has none.
All inputs are finite; a program needn't handle non-finite values.
Results may differ from the reference program's by a relative error of at most 0.0045.
Values may be sent and summed in bfloat16 or wider, within the bound.
A program may use at most 128 MiB of HBM per device.

```python
import math
import jax
import jax.numpy as jnp
from jax import lax

D = 512
HEADS = 4
BITS = 8
OCTANTS = 8
NODE_DEV = 512
PAR_DEV = 256
NODES = 65536
PARENTS = 32768


def draw_parent_rows(key, part):
    own_key = jax.random.fold_in(key, 11)
    first, second, third = jax.random.split(own_key, 3)
    base = jnp.clip(jax.random.normal(first, (PARENTS, D), jnp.float32), -5.0, 5.0)
    row_scale = jnp.exp(jax.random.uniform(second, (PARENTS, 1), jnp.float32, 0.0, math.log(10.0)))
    col_scale = jnp.exp(jax.random.uniform(third, (1, D), jnp.float32, 0.0, math.log(10.0)))
    return (base * row_scale * col_scale * 0.1).astype(jnp.bfloat16)


def draw_counts(key, part):
    own_key = jax.random.fold_in(key, 23)
    blocks = PARENTS // PAR_DEV
    quarter = NODE_DEV // 4
    first, second, third = jax.random.split(own_key, 3)
    excess = jax.random.randint(first, (blocks,), -quarter, quarter + 1).astype(jnp.int32)
    places = jnp.arange(blocks)
    excess = jnp.where(places == 0, quarter, jnp.where(places == 1, -quarter, excess))
    excess = jnp.where(places == blocks - 1, 0, excess).astype(jnp.int32)
    before = jnp.concatenate([jnp.zeros((1,), jnp.int32), excess[:-1]])
    totals = NODE_DEV + excess - before
    full_bins = jax.random.randint(second, (blocks,), 0, PAR_DEV).astype(jnp.int32)
    block_keys = jax.random.split(third, blocks)
    slots = 8 * PAR_DEV

    def one_block(block_key, total, full_bin):
        ranks = jax.random.permutation(block_key, slots).astype(jnp.int32)
        bin_of = jnp.arange(slots, dtype=jnp.int32) // 8
        empty_bin = (full_bin + 1) % PAR_DEV
        special = (bin_of == full_bin) | (bin_of == empty_bin)
        taken = jnp.concatenate([jax.lax.dynamic_slice_in_dim(ranks, full_bin * 8, 8), jax.lax.dynamic_slice_in_dim(ranks, empty_bin * 8, 8)])
        below = jnp.sum((taken[None, :] < ranks[:, None]).astype(jnp.int32), axis=1)
        other_rank = ranks - below
        chosen = (bin_of == full_bin) | jnp.logical_not(special) & (other_rank < total - 8)
        return jnp.sum(chosen.reshape(PAR_DEV, 8).astype(jnp.int32), axis=1)
    return jax.vmap(one_block)(block_keys, totals, full_bins).reshape(PARENTS).astype(jnp.int32)


def set_ends(entries, stream_key, low, high):
    place = [jax.random.randint(jax.random.fold_in(stream_key, axis), (), 0, length) for axis, length in enumerate(entries.shape)]
    longest = entries.shape.index(max(entries.shape))
    next_to = place[:longest] + [(place[longest] + 1) % entries.shape[longest]] + place[longest + 1:]
    return entries.at[tuple(place)].set(low).at[tuple(next_to)].set(high)


def bell_draw(key, shape, deviation, reach, held_as=jnp.bfloat16):
    return jnp.clip(deviation * jax.random.normal(key, shape, jnp.float32), -reach, reach).astype(held_as)


def setup_inputs(seed: int = 0) -> dict:
    seeds = jax.random.split(jax.random.key(seed), 9)
    return {
        "parent_rows": draw_parent_rows(jax.random.fold_in(seeds[8], 71), 0),
        "counts": draw_counts(jax.random.fold_in(seeds[8], 71), 0),
        "occupancy": set_ends(jax.random.randint(seeds[2], (NODES,), 1, 256), jax.random.fold_in(seeds[2], 1), 1, 255).astype(jnp.int32),
        "sib_table": bell_draw(seeds[3], (OCTANTS, D), 1.0, 6.0),
        "gain": jnp.clip(1.0 + 0.18 * jax.random.normal(seeds[4], (D,), jnp.float32), 0.1, 1.9),
        "w_qkv": bell_draw(seeds[5], (D, 3 * D), D ** -0.5, 0.25),
        "w_out": bell_draw(seeds[6], (D, D), D ** -0.5, 0.25),
        "w_head": bell_draw(seeds[7], (D, BITS), D ** -0.5, 0.25),
    }


highest = lax.Precision.HIGHEST

def head_slice(packed, part, head_id, width):
    head_size = width // HEADS
    begin = part * width + head_id * head_size
    return packed[:, begin:begin + head_size]

def normalize_inputs(inputs, gain):
    inputs_f = inputs.astype(jnp.float32)
    inv_in = lax.rsqrt(lax.optimization_barrier(jnp.mean(inputs_f * inputs_f, axis=-1, keepdims=True)) + 1e-06)
    normed = (inputs_f * inv_in * gain).astype(jnp.bfloat16)
    return (inputs_f, inv_in, normed)

def local_states(packed, width):
    return jnp.stack([jnp.dot(head_slice(packed, 1, head_id, width).T, head_slice(packed, 2, head_id, width), preferred_element_type=jnp.float32) for head_id in range(HEADS)])

def query_states(packed, grads, width):
    return jnp.stack([jnp.dot(head_slice(packed, 0, head_id, width).T, grads[head_id], preferred_element_type=jnp.float32) for head_id in range(HEADS)])

def causal_mask(count):
    return jnp.tril(jnp.ones((count, count), jnp.bool_))

def attend(packed, prefix, width):
    causal = causal_mask(packed.shape[0])
    scores = []
    numers = []
    inverses = []
    pieces = []
    for head_id in range(HEADS):
        queries = head_slice(packed, 0, head_id, width)
        keys_here = head_slice(packed, 1, head_id, width)
        values_here = head_slice(packed, 2, head_id, width)
        score = jnp.where(causal, jnp.dot(queries, keys_here.T, preferred_element_type=jnp.float32), 0.0)
        numer = jnp.dot(score, values_here.astype(jnp.float32), precision=highest) + jnp.dot(queries.astype(jnp.float32), prefix[head_id], precision=highest)
        inverse = lax.rsqrt(lax.optimization_barrier(jnp.mean(numer * numer, axis=-1, keepdims=True)) + 1e-05)
        scores.append(score)
        numers.append(numer)
        inverses.append(inverse)
        pieces.append(numer * inverse)
    attended = jnp.concatenate(pieces, axis=1).astype(jnp.bfloat16)
    return (scores, numers, inverses, attended)

def readout(inputs_f, attended, w_out, w_head):
    resid = inputs_f + jnp.dot(attended, w_out, preferred_element_type=jnp.float32)
    inv_out = lax.rsqrt(lax.optimization_barrier(jnp.mean(resid * resid, axis=-1, keepdims=True)) + 1e-06)
    final = (resid * inv_out).astype(jnp.bfloat16)
    logits = jnp.dot(final, w_head, preferred_element_type=jnp.float32)
    return (resid, inv_out, final, logits)

def output_grads(occupancy, logits, final, resid, inv_out, w_head, scale):
    powers = 2 ** jnp.arange(w_head.shape[1], dtype=jnp.int32)
    target = (occupancy[:, None] // powers[None, :] % 2).astype(jnp.float32)
    d_logits = ((jax.nn.sigmoid(logits) - target) * scale).astype(jnp.bfloat16)
    grad_head = jnp.dot(final.T, d_logits, preferred_element_type=jnp.float32)
    d_final = jnp.dot(d_logits, w_head.T, preferred_element_type=jnp.float32)
    d_resid = inv_out * d_final - resid * inv_out ** 3 * lax.optimization_barrier(jnp.mean(d_final * resid, axis=-1, keepdims=True))
    return (grad_head, d_resid)

def numer_grads(attended, d_resid, numers, inverses, w_out, width):
    d_resid_b = d_resid.astype(jnp.bfloat16)
    grad_out = jnp.dot(attended.T, d_resid_b, preferred_element_type=jnp.float32)
    d_attended = jnp.dot(d_resid_b, w_out.T, preferred_element_type=jnp.float32)
    head_size = width // HEADS
    grads = []
    for head_id in range(HEADS):
        piece = d_attended[:, head_id * head_size:(head_id + 1) * head_size]
        numer = numers[head_id]
        inverse = inverses[head_id]
        d_numer = inverse * piece - numer * inverse ** 3 * lax.optimization_barrier(jnp.mean(piece * numer, axis=-1, keepdims=True))
        grads.append(d_numer.astype(jnp.bfloat16))
    return (grad_out, grads)

def attention_grads(packed, scores, grads, prefix, suffix, width):
    causal = causal_mask(packed.shape[0])
    d_queries = []
    d_keys = []
    d_values = []
    for head_id in range(HEADS):
        queries = head_slice(packed, 0, head_id, width)
        keys_here = head_slice(packed, 1, head_id, width)
        values_here = head_slice(packed, 2, head_id, width)
        grad = grads[head_id]
        grad_f = grad.astype(jnp.float32)
        back = jnp.where(causal, jnp.dot(grad, values_here.T, preferred_element_type=jnp.float32), 0.0)
        d_queries.append(jnp.dot(back, keys_here.astype(jnp.float32), precision=highest) + jnp.dot(grad_f, prefix[head_id].T, precision=highest))
        d_keys.append(jnp.dot(back.T, queries.astype(jnp.float32), precision=highest) + jnp.dot(values_here.astype(jnp.float32), suffix[head_id].T, precision=highest))
        d_values.append(jnp.dot(scores[head_id].T, grad_f, precision=highest) + jnp.dot(keys_here.astype(jnp.float32), suffix[head_id], precision=highest))
    return jnp.concatenate(d_queries + d_keys + d_values, axis=1).astype(jnp.bfloat16)

def input_grads(inputs_f, inv_in, normed, d_packed, d_resid, onehot, gain, w_qkv):
    grad_qkv = jnp.dot(normed.T, d_packed, preferred_element_type=jnp.float32)
    d_normed = jnp.dot(d_packed, w_qkv.T, preferred_element_type=jnp.float32)
    grad_gain = lax.optimization_barrier(jnp.sum(d_normed * inputs_f * inv_in, axis=0))
    d_scaled = d_normed * gain
    d_inputs = inv_in * d_scaled - inputs_f * inv_in ** 3 * lax.optimization_barrier(jnp.mean(d_scaled * inputs_f, axis=-1, keepdims=True)) + d_resid
    grad_sib = jnp.dot(onehot.T, d_inputs, precision=highest)
    return (grad_qkv, grad_gain, grad_sib)

def reference(parent_rows, counts, occupancy, sib_table, gain, w_qkv, w_out, w_head):
    width = parent_rows.shape[1]
    ends = jnp.cumsum(counts).astype(jnp.int32)
    starts = ends - counts
    node_ids = jnp.arange(NODES, dtype=jnp.int32)
    parent_of = jnp.searchsorted(ends, node_ids, side='right').astype(jnp.int32)
    rank = node_ids - starts[parent_of]
    onehot = (rank[:, None] == jnp.arange(sib_table.shape[0], dtype=jnp.int32)[None, :]).astype(jnp.float32)
    inputs = (parent_rows[parent_of].astype(jnp.float32) + jnp.dot(onehot.astype(jnp.bfloat16), sib_table, preferred_element_type=jnp.float32)).astype(jnp.bfloat16)
    blocks = NODES // NODE_DEV
    inputs_b = inputs.reshape(blocks, NODE_DEV, width)
    onehot_b = onehot.reshape(blocks, NODE_DEV, onehot.shape[1])
    occupancy_b = occupancy.reshape(blocks, NODE_DEV)
    scale = float(NODES) ** (-0.5)

    def first_pass(block):
        inputs_f, inv_in, normed = normalize_inputs(block, gain)
        packed = jnp.dot(normed, w_qkv, preferred_element_type=jnp.float32).astype(jnp.bfloat16)
        return (packed, local_states(packed, width))
    packed_b, states_b = lax.map(first_pass, inputs_b)
    prefix_b = jnp.concatenate([jnp.zeros_like(states_b[:1]), jnp.cumsum(states_b, axis=0)[:-1]], axis=0)

    def second_pass(items):
        block, packed, prefix, occ = items
        inputs_f, inv_in, normed = normalize_inputs(block, gain)
        scores, numers, inverses, attended = attend(packed, prefix, width)
        resid, inv_out, final, logits = readout(inputs_f, attended, w_out, w_head)
        grad_head, d_resid = output_grads(occ, logits, final, resid, inv_out, w_head, scale)
        grad_out, grads = numer_grads(attended, d_resid, numers, inverses, w_out, width)
        return (grad_head, grad_out, d_resid, jnp.stack(grads), query_states(packed, grads, width))
    head_b, out_b, resid_grad_b, grads_b, qstates_b = lax.map(second_pass, (inputs_b, packed_b, prefix_b, occupancy_b))
    suffix_b = jnp.concatenate([jnp.cumsum(qstates_b[::-1], axis=0)[::-1][1:], jnp.zeros_like(qstates_b[:1])], axis=0)

    def third_pass(carry, items):
        block, packed, prefix, suffix, grads, d_resid, onehot_here = items
        inputs_f, inv_in, normed = normalize_inputs(block, gain)
        scores, numers, inverses, attended = attend(packed, prefix, width)
        d_packed = attention_grads(packed, scores, grads, prefix, suffix, width)
        parts = input_grads(inputs_f, inv_in, normed, d_packed, d_resid, onehot_here, gain, w_qkv)
        return ((carry[0] + parts[0], carry[1] + parts[1], carry[2] + parts[2]), None)
    start = (jnp.zeros((width, 3 * width), jnp.float32), jnp.zeros((width,), jnp.float32), jnp.zeros((sib_table.shape[0], width), jnp.float32))
    totals, unused = lax.scan(third_pass, start, (inputs_b, packed_b, prefix_b, suffix_b, grads_b, resid_grad_b, onehot_b))
    return (totals[0], lax.optimization_barrier(jnp.sum(out_b, axis=0)), lax.optimization_barrier(jnp.sum(head_b, axis=0)), totals[1], totals[2])
```

```python
import jax
import jax.numpy as jnp
from jax import lax
from jax.experimental import pallas as pl
from jax.experimental.pallas import tpu as pltpu
from jax.sharding import PartitionSpec as P

MESH = pl.DeviceIdType.MESH
F32, BF16 = jnp.float32, jnp.bfloat16
HEADS, HS, D = 4, 128, 512
N, PAR, DEVS = 512, 256, 128
RB = 128
BLOCKS = N // RB
COPIES = 160
PLANE = [(dx, dy) for dx in range(4) for dy in range(4) if dx or dy]


def dot(a, b):
    return jnp.dot(a, b, preferred_element_type=F32)


def dot_tn(a, b):
    return lax.dot_general(a, b, (((0,), (0,)), ((), ())), preferred_element_type=F32)


def dot_nt(a, b):
    return lax.dot_general(a, b, (((1,), (1,)), ((), ())), preferred_element_type=F32)


def split(value):
    high = value.astype(BF16)
    return high, (value - high.astype(F32)).astype(BF16)


def rows(start, count):
    return pl.ds(pl.multiple_of(start, count), count)


class Place:
    def __init__(self):
        me = lax.axis_index("seq")
        self.me = me
        self.x, self.y, self.z, self.c = me // 32, (me // 8) % 4, (me // 2) % 4, me % 2
        self.g = self.x * 4 + self.y
        self.sibling = me + 1 - 2 * self.c
        self.next = (me + 1) % DEVS
        self.prev = (me + DEVS - 1) % DEVS

    def line(self):
        for d in (1, 2, 3):
            zt = (self.z + d) % 4
            yield zt, self.me - 2 * self.z + 2 * zt

    def plane(self):
        for dx, dy in PLANE:
            xt, yt = (self.x + dx) % 4, (self.y + dy) % 4
            yield xt, yt, (xt * 4 + yt) * 8 + self.me % 8


class Links:
    def __init__(self, send, recv):
        self.send, self.recv, self.sent = send, recv, []

    def start(self, src, dst, device):
        k = len(self.sent)
        copy = pltpu.make_async_remote_copy(
            src_ref=src,
            dst_ref=dst,
            send_sem=self.send.at[k],
            recv_sem=self.recv.at[k],
            device_id=(device,),
            device_id_type=MESH,
        )
        copy.start()
        self.sent.append(copy)
        return copy

    def finish(self):
        for copy in self.sent:
            copy.wait_send()


def arrived(copies):
    for copy in copies:
        copy.wait_recv()


def greet(at):
    barrier = pltpu.get_barrier_semaphore()
    far = at.me + DEVS - 1 + 2 * at.c
    partners = [at.sibling, far % DEVS]
    partners += [dev for zt, dev in at.line()] + [dev for xt, yt, dev in at.plane()]
    for dev in partners:
        pl.semaphore_signal(barrier, inc=1, device_id=(dev,), device_id_type=MESH)
    pl.semaphore_wait(barrier, len(partners))


def scan(at, links, state, out, sib, chip, zbuf, pbuf, ret, ebuf, give, reverse):
    mine, other = rows(at.c * 256, 256), rows((1 - at.c) * 256, 256)
    first = links.start(state.at[other], sib, at.sibling)
    yield
    arrived([first])
    chip[...] = state[mine, :] + sib[...]
    copies = []
    for zt, dev in at.line():
        copies.append(links.start(chip.at[rows(zt * 64, 64)], zbuf.at[at.z], dev))
    zbuf[at.z] = chip[rows(at.z * 64, 64), :]
    yield
    arrived(copies)
    pbuf[at.g] = zbuf[0] + zbuf[1] + zbuf[2] + zbuf[3]
    copies = []
    for xt, yt, dev in at.plane():
        copies.append(links.start(pbuf.at[at.g], pbuf.at[at.g], dev))
    yield
    arrived(copies)
    total = jnp.zeros((64, HS), F32)
    for k in range(16):
        passed = (k > at.g) if reverse else (k < at.g)
        total = total + jnp.where(passed, pbuf[k], 0.0)
    for k in range(3, -1, -1) if reverse else range(4):
        ret[k] = total
        total = total + zbuf[k]
    copies = []
    for zt, dev in at.line():
        copies.append(links.start(ret.at[zt], ebuf.at[at.z], dev))
    ebuf[at.z] = ret[at.z]
    yield
    arrived(copies)
    first_core = at.c == (1 if reverse else 0)
    before = ebuf[...].reshape(256, HS)
    give[...] = before + jnp.where(first_core, state[mine, :], 0.0)
    last = links.start(give, out.at[mine], at.sibling)
    out[mine, :] = before + jnp.where(first_core, 0.0, sib[...])
    yield
    arrived([last])


def reduce_all(at, links, src, out, r0, r1, zb, r2, pb, small=None):
    mine, other = rows(at.c * 256, 256), rows((1 - at.c) * 256, 256)
    copies = [links.start(src.at[other], r0, at.sibling)]
    if small:
        xs, xo, x0, x1, xz = small
        xmine, xother = rows(at.c * 16, 16), rows((1 - at.c) * 16, 16)
        copies.append(links.start(xs.at[xother], x0, at.sibling))
    yield
    arrived(copies)
    for k in range(4):
        part = pl.ds(k * 64, 64)
        r1[part, :] = src[rows(at.c * 256 + k * 64, 64), :] + r0[part, :]
    copies = []
    if small:
        total = xs[xmine, :] + x0[...]
        for k in range(4):
            x1[k] = total[:, k * 128 : (k + 1) * 128]
        for zt, dev in at.line():
            copies.append(links.start(x1.at[zt], xz.at[at.z], dev))
        xz[at.z] = x1[at.z]
    for zt, dev in at.line():
        copies.append(links.start(r1.at[rows(zt * 64, 64)], zb.at[at.z], dev))
    yield
    arrived(copies)
    width = 384 if small else 256
    own = at.z * 64
    for k in range(16):
        xk, yk = k // 4, k % 4
        cols = pl.ds(yk * 256, 256)
        value = jnp.zeros((16, 256), F32)
        for j in range(4):
            piece = jnp.where(j == at.z, r1[rows(own + xk * 16, 16), cols], zb[j, pl.ds(xk * 16, 16), cols])
            value = value + piece
        r2[k, :, pl.ds(0, 256)] = value
    if small:
        value = xz[0] + xz[1] + xz[2] + xz[3]
        for k in range(16):
            r2[k, :, pl.ds(256, 128)] = value
    copies = []
    for xt, yt, dev in at.plane():
        copies.append(links.start(r2.at[xt * 4 + yt], pb.at[at.g], dev))
    pb[at.g] = r2[at.g]
    yield
    arrived(copies)
    total = pb[0]
    for k in range(1, 16):
        total = total + pb[k]
    place = out.at[rows(at.c * 256 + own + at.x * 16, 16), rows(at.y * 256, 256)]
    place[...] = total[:, :256]
    copies = []
    for xt, yt, dev in at.plane():
        copies.append(links.start(place, place, dev))
    if small:
        xplace = xo.at[xmine, rows(at.z * 128, 128)]
        xplace[...] = total[:, 256:]
        for zt, dev in at.line():
            copies.append(links.start(xplace, xplace, dev))
    yield
    arrived(copies)
    place = out.at[rows(at.c * 256 + own, 64)]
    copies = []
    for zt, dev in at.line():
        copies.append(links.start(place, place, dev))
    if small:
        copies.append(links.start(xo.at[xmine], xo.at[xmine], at.sibling))
    yield
    arrived(copies)
    last = links.start(out.at[mine], out.at[mine], at.sibling)
    yield
    arrived([last])


def step(generator):
    for _ in generator:
        return True
    return False


def finish(generator):
    while step(generator):
        pass


def head(h, part=0):
    return pl.ds(part * D + h * HS, HS)


def block(b):
    return pl.ds(b * RB, RB)


def lower(b):
    row = lax.broadcasted_iota(jnp.int32, (RB, (b + 1) * RB), 0) + b * RB
    col = lax.broadcasted_iota(jnp.int32, (RB, (b + 1) * RB), 1)
    return col <= row


def kernel(
    parents, counts, occupancy, sib_table, gain, w_qkv, w_out, w_head,
    early_out, late_out, small_out,
    window, ends, offz, offp, offs, inputs, inv_in, normed, packed, onehot,
    scores, numer, resid, inv_out, final, attended, d_logits, d_resid, d_resid_b, wide, grads, d_packed,
    d_local, states, prefix, qstates, suffix,
    f_sib, f_chip, f_z, f_p, f_ret, f_e, f_give,
    b_sib, b_chip, b_z, b_p, b_ret, b_e, b_give,
    early, e_r0, e_r1, e_z, e_r2, e_p,
    late, l_r0, l_r1, l_z, l_r2, l_p,
    small, x0, x1, xz,
    send, recv,
):
    at = Place()
    links = Links(send, recv)
    greet(at)

    own = pl.ds(PAR, PAR)
    tri = (
        lax.broadcasted_iota(jnp.int32, (PAR, PAR), 0) <= lax.broadcasted_iota(jnp.int32, (PAR, PAR), 1)
    ).astype(BF16)
    count = jnp.broadcast_to(counts[...].astype(F32), (16, PAR))
    local_ends = dot(count.astype(BF16), tri)[:8]
    whole = jnp.sum(count[:8], axis=1, keepdims=True)
    ends[1, :8] = local_ends
    ends[1, 8:] = count[:8]
    halo = [
        links.start(ends.at[1], ends.at[0], at.next),
        links.start(ends.at[1], ends.at[2], at.prev),
        links.start(parents, window.at[pl.ds(0, PAR)], at.next),
        links.start(parents, window.at[pl.ds(2 * PAR, PAR)], at.prev),
    ]
    window[own, :] = parents[...]

    offs[0] = jnp.broadcast_to(whole, (8, 128))
    first = links.start(offs.at[0], offs.at[1], at.sibling)
    arrived([first])
    offset = jnp.where(at.c == 1, offs[1], 0.0)
    offz[at.z] = offs[0] + offs[1]
    copies = [links.start(offz.at[at.z], offz.at[at.z], dev) for zt, dev in at.line()]
    arrived(copies)
    offp[at.g] = offz[0] + offz[1] + offz[2] + offz[3]
    copies = [links.start(offp.at[at.g], offp.at[at.g], dev) for xt, yt, dev in at.plane()]
    for k in range(4):
        offset = offset + jnp.where(k < at.z, offz[k], 0.0)
    arrived(copies)
    for k in range(16):
        offset = offset + jnp.where(k < at.g, offp[k], 0.0)
    shift = (at.me * N).astype(F32) - offset[:1, :1]

    arrived(halo)
    own_total = whole[:1, :1]
    low_total = ends[0, :1, PAR - 1 :]
    end_row = jnp.concatenate([ends[0, :1] - low_total, local_ends[:1], ends[2, :1] + own_total], axis=1)
    count_row = jnp.concatenate([ends[0, 8:9], count[:1], ends[2, 8:9]], axis=1)
    start_row = end_row - count_row
    lanes8 = lax.broadcasted_iota(jnp.int32, (128, 8), 0)
    spread = (lanes8 == lax.broadcasted_iota(jnp.int32, (128, 8), 1) + 16).astype(BF16)
    sib_rows = dot(spread, sib_table[...]).astype(BF16)
    lane = lax.broadcasted_iota(jnp.int32, (RB, 128), 1)
    for b in range(BLOCKS):
        place = lax.broadcasted_iota(jnp.int32, (RB, 1), 0).astype(F32) + (shift + float(b * RB))
        child = (start_row <= place) & (place < end_row)
        chosen = jnp.where(child, 1.0, 0.0).astype(BF16)
        start_of = jnp.sum(jnp.where(child, start_row, 0.0), axis=1, keepdims=True)
        rank = (place - start_of).astype(jnp.int32)
        hot = (rank + 16 == lane).astype(F32).astype(BF16)
        onehot[block(b), :] = hot
        value = (dot(chosen, window[...]) + dot(hot, sib_rows)).astype(BF16)
        inputs[block(b), :] = value
        value = value.astype(F32)
        inverse = lax.rsqrt(jnp.mean(value * value, axis=-1, keepdims=True) + 1e-06)
        inv_in[block(b), :] = inverse
        normed[block(b), :] = (value * inverse * gain[...]).astype(BF16)
    packed[...] = dot(normed[...], w_qkv[...]).astype(BF16)
    for h in range(HEADS):
        states[pl.ds(h * HS, HS), :] = dot_tn(packed[:, head(h, 1)], packed[:, head(h, 2)])

    forward = scan(at, links, states, prefix, f_sib, f_chip, f_z, f_p, f_ret, f_e, f_give, False)
    step(forward)
    for h in range(HEADS):
        for b in range(BLOCKS):
            keys, values = packed[: (b + 1) * RB, head(h, 1)], packed[: (b + 1) * RB, head(h, 2)]
            score = jnp.where(lower(b), dot_nt(packed[block(b), head(h)], keys), 0.0).astype(BF16)
            scores[h, block(b), : (b + 1) * RB] = score
            numer[block(b), head(h)] = dot(score, values)
        step(forward)
    finish(forward)

    for h in range(HEADS):
        high, low = split(prefix[pl.ds(h * HS, HS), :])
        q = packed[:, head(h)]
        wide[:, head(h)] = dot(q, high) + dot(q, low)
    scale = float(DEVS * N) ** (-0.5)
    lane8 = lax.broadcasted_iota(jnp.int32, (RB, 8), 1)
    inv_heads = []
    for b in range(BLOCKS):
        for h in range(HEADS):
            value = numer[block(b), head(h)] + wide[block(b), head(h)]
            numer[block(b), head(h)] = value
            inverse = lax.rsqrt(jnp.mean(value * value, axis=-1, keepdims=True) + 1e-05)
            attended[block(b), head(h)] = (value * inverse).astype(BF16)
            inv_heads.append(inverse)
    wide[...] = dot(attended[...], w_out[...])
    for b in range(BLOCKS):
        value = inputs[block(b), :].astype(F32) + wide[block(b), :]
        resid[block(b), :] = value
        inverse = lax.rsqrt(jnp.mean(value * value, axis=-1, keepdims=True) + 1e-06)
        inv_out[block(b), :] = inverse
        last = (value * inverse).astype(BF16)
        final[block(b), :] = last
        logits = dot(last, w_head[...])
        target = ((occupancy[block(b), :] >> lane8) & 1).astype(F32)
        small_grad = ((jax.nn.sigmoid(logits) - target) * scale).astype(BF16)
        d_logits[block(b), :] = small_grad
        d_final = dot_nt(small_grad, w_head[...])
        mean = jnp.mean(d_final * value, axis=-1, keepdims=True)
        d_value = inverse * d_final - value * (inverse * inverse * inverse) * mean
        d_resid[block(b), :] = d_value
        d_resid_b[block(b), :] = d_value.astype(BF16)
    wide[...] = dot_nt(d_resid_b[...], w_out[...])
    for b in range(BLOCKS):
        for h in range(HEADS):
            piece, value, inverse = wide[block(b), head(h)], numer[block(b), head(h)], inv_heads[b * HEADS + h]
            mean = jnp.mean(piece * value, axis=-1, keepdims=True)
            grads[block(b), head(h)] = (inverse * piece - value * (inverse * inverse * inverse) * mean).astype(BF16)
    for h in range(HEADS):
        qstates[pl.ds(h * HS, HS), :] = dot_tn(packed[:, head(h)], grads[:, head(h)])

    backward = scan(at, links, qstates, suffix, b_sib, b_chip, b_z, b_p, b_ret, b_e, b_give, True)
    step(backward)
    early[:, pl.ds(0, D)] = dot_tn(attended[...], d_resid_b[...])
    step(backward)
    for h in range(HEADS):
        high, low = split(prefix[pl.ds(h * HS, HS), :])
        g = grads[:, head(h)]
        wide[:, head(h)] = dot_nt(g, high) + dot_nt(g, low)
    d_local[...] = jnp.zeros_like(d_local)
    for h in range(HEADS):
        for b in range(BLOCKS):
            upto = pl.ds(0, (b + 1) * RB)
            g, q = grads[block(b), head(h)], packed[block(b), head(h)]
            back = jnp.where(lower(b), dot_nt(g, packed[upto, head(h, 2)]), 0.0).astype(BF16)
            dq = dot(back, packed[upto, head(h, 1)]) + wide[block(b), head(h)]
            d_packed[block(b), head(h)] = dq.astype(BF16)
            d_local[upto, head(h)] += dot_tn(back, q)
            d_local[upto, head(h, 1)] += dot_tn(scores[h, block(b), upto], g)
        if h == 1:
            step(backward)
    early[:, pl.ds(D, D)] = dot_tn(normed[...], d_packed[:, pl.ds(0, D)])
    early_sum = reduce_all(at, links, early, early_out, e_r0, e_r1, e_z, e_r2, e_p)
    step(early_sum)
    wide[...] = dot_nt(d_packed[:, pl.ds(0, D)], w_qkv[:, pl.ds(0, D)])
    step(backward)
    finish(backward)
    step(early_sum)

    for h in range(HEADS):
        high, low = split(suffix[pl.ds(h * HS, HS), :])
        k, v = packed[:, head(h, 1)], packed[:, head(h, 2)]
        d_packed[:, head(h, 1)] = (d_local[:, head(h)] + dot_nt(v, high) + dot_nt(v, low)).astype(BF16)
        d_packed[:, head(h, 2)] = (d_local[:, head(h, 1)] + dot(k, high) + dot(k, low)).astype(BF16)
    late[...] = dot_tn(normed[...], d_packed[:, pl.ds(D, 2 * D)])
    wide[...] += dot_nt(d_packed[:, pl.ds(D, 2 * D)], w_qkv[:, pl.ds(D, 2 * D)])
    step(early_sum)
    grad_gain = jnp.zeros((1, D), F32)
    grad_sib = jnp.zeros((128, D), F32)
    for b in range(BLOCKS):
        value, inverse, slope = inputs[block(b), :].astype(F32), inv_in[block(b), :], wide[block(b), :]
        grad_gain = grad_gain + jnp.sum(slope * value * inverse, axis=0, keepdims=True)
        scaled = slope * gain[...]
        mean = jnp.mean(scaled * value, axis=-1, keepdims=True)
        d_in = inverse * scaled - value * (inverse * inverse * inverse) * mean + d_resid[block(b), :]
        high, low = split(d_in)
        grad_sib = grad_sib + dot_tn(onehot[block(b), :], high) + dot_tn(onehot[block(b), :], low)
    small[pl.ds(0, 8), :] = dot_tn(d_logits[...], final[...])
    small[pl.ds(8, 8), :] = jnp.broadcast_to(grad_gain, (8, D))
    small[pl.ds(16, 16), :] = grad_sib[16:32]
    late_sum = reduce_all(at, links, late, late_out, l_r0, l_r1, l_z, l_r2, l_p, (small, small_out, x0, x1, xz))
    step(late_sum)
    step(early_sum)
    more = True
    while more:
        more = step(late_sum)
        step(early_sum)
    finish(early_sum)
    links.finish()


def vm(shape, dtype=F32):
    return pltpu.VMEM(shape, dtype)


def scan_buffers():
    return [vm((256, HS)), vm((256, HS)), vm((4, 64, HS)), vm((16, 64, HS)), vm((4, 64, HS)), vm((4, 64, HS)), vm((256, HS))]


def sum_buffers(width):
    return [vm((N, 1024)), vm((256, 1024)), vm((256, 1024)), vm((4, 64, 1024)), vm((16, 16, width)), vm((16, 16, width))]


def shards(parent_rows, counts, occupancy, sib_table, gain, w_qkv, w_out, w_head):
    scratch = [
        vm((3 * PAR, D), BF16), vm((3, 16, PAR)), vm((4, 8, 128)), vm((16, 8, 128)), vm((2, 8, 128)),
        vm((N, D), BF16), vm((N, 1)), vm((N, D), BF16), vm((N, 3 * D), BF16), vm((N, 128), BF16),
        vm((HEADS, N, N), BF16), vm((N, D)), vm((N, D)), vm((N, 1)), vm((N, D), BF16), vm((N, D), BF16),
        vm((N, 8), BF16), vm((N, D)), vm((N, D), BF16), vm((N, D)), vm((N, D), BF16), vm((N, 3 * D), BF16),
        vm((N, 2 * D)), vm((N, HS)), vm((N, HS)), vm((N, HS)), vm((N, HS)),
        *scan_buffers(), *scan_buffers(), *sum_buffers(256), *sum_buffers(384),
        vm((32, D)), vm((16, D)), vm((4, 16, 128)), vm((4, 16, 128)),
        pltpu.SemaphoreType.DMA((COPIES,)), pltpu.SemaphoreType.DMA((COPIES,)),
    ]
    spec = pl.BlockSpec(memory_space=pltpu.VMEM)
    early, late, small = pl.pallas_call(
        kernel,
        out_shape=[
            jax.ShapeDtypeStruct((D, 1024), F32),
            jax.ShapeDtypeStruct((D, 1024), F32),
            jax.ShapeDtypeStruct((32, D), F32),
        ],
        in_specs=[spec] * 8,
        out_specs=[spec] * 3,
        scratch_shapes=scratch,
        compiler_params=pltpu.CompilerParams(
            collective_id=0, has_side_effects=True, vmem_limit_bytes=60 * 1024 * 1024
        ),
        name="train_step",
    )(
        parent_rows, counts.reshape(1, PAR), occupancy.reshape(N, 1), sib_table, gain.reshape(1, D),
        w_qkv, w_out, w_head,
    )
    grad_qkv = jnp.concatenate([early[:, D:], late], axis=1)
    return grad_qkv, early[:, :D], small[:8].T, small[8], small[16:24]


def solution(mesh):
    placed = (P("seq", None), P("seq"), P("seq"), P(), P(), P(), P(), P())
    return jax.shard_map(
        shards, mesh=mesh, in_specs=placed, out_specs=(P(), P(), P(), P(), P()), check_vma=False
    )
```

```python
import jax
import jax.numpy as jnp
from jax import lax
from jax.experimental import pallas as pl
from jax.experimental.pallas import tpu as pltpu
from jax.sharding import PartitionSpec as P

MESH = pl.DeviceIdType.MESH
F32, BF16 = jnp.float32, jnp.bfloat16
HEADS, HS, D = 4, 128, 512
N, PAR, DEVS = 512, 256, 128
RB = 128
BLOCKS = N // RB
COPIES = 184
PLANE = [(dx, dy) for dx in range(4) for dy in range(4) if dx or dy]


def dot(a, b):
    return jnp.dot(a, b, preferred_element_type=F32)


def dot_tn(a, b):
    return lax.dot_general(a, b, (((0,), (0,)), ((), ())), preferred_element_type=F32)


def dot_nt(a, b):
    return lax.dot_general(a, b, (((1,), (1,)), ((), ())), preferred_element_type=F32)


def split(value):
    high = value.astype(BF16)
    return high, (value - high.astype(F32)).astype(BF16)


def rows(start, count):
    return pl.ds(pl.multiple_of(start, count), count)


class Place:
    def __init__(self):
        me = lax.axis_index("seq")
        self.me = me
        self.x, self.y, self.z, self.c = me // 32, (me // 8) % 4, (me // 2) % 4, me % 2
        self.g = self.x * 4 + self.y
        self.sibling = me + 1 - 2 * self.c
        c = self.c
        self.l, self.l_step = self.z + c * (self.x - self.z), 2 + 30 * c
        self.p, self.p_step = self.x + c * (self.y - self.x), 32 - 24 * c
        self.q, self.q_step = self.y + c * (self.z - self.y), 8 - 6 * c
        self.l_sibling = self.x + c * (self.z - self.x)
        self.pq = self.p * 4 + self.q
        self.next = (me + 1) % DEVS
        self.prev = (me + DEVS - 1) % DEVS

    def line(self):
        for d in (1, 2, 3):
            zt = (self.z + d) % 4
            yield zt, self.me - 2 * self.z + 2 * zt

    def plane(self):
        for dx, dy in PLANE:
            xt, yt = (self.x + dx) % 4, (self.y + dy) % 4
            yield xt, yt, (xt * 4 + yt) * 8 + self.me % 8


    def sum_line(self):
        for d in (1, 2, 3):
            lt = (self.l + d) % 4
            yield lt, self.me + (lt - self.l) * self.l_step

    def sum_plane(self):
        for dp, dq in PLANE:
            pt, qt = (self.p + dp) % 4, (self.q + dq) % 4
            yield pt * 4 + qt, self.me + (pt - self.p) * self.p_step + (qt - self.q) * self.q_step


class Links:
    def __init__(self, send, recv):
        self.send, self.recv, self.sent = send, recv, []

    def start(self, src, dst, device, when=None):
        k = len(self.sent)
        copy = pltpu.make_async_remote_copy(
            src_ref=src,
            dst_ref=dst,
            send_sem=self.send.at[k],
            recv_sem=self.recv.at[k],
            device_id=(device,),
            device_id_type=MESH,
        )
        if when is None:
            copy.start()
        else:
            pl.when(when)(copy.start)
        self.sent.append((copy, when))
        return copy

    def finish(self):
        for copy, when in self.sent:
            if when is None:
                copy.wait_send()
            else:
                pl.when(when)(copy.wait_send)


def arrived(copies):
    for copy in copies:
        copy.wait_recv()


def greet(at):
    barrier = pltpu.get_barrier_semaphore()
    far = at.me + DEVS - 1 + 2 * at.c
    partners = [at.sibling, far % DEVS]
    partners += [dev for zt, dev in at.line()] + [dev for xt, yt, dev in at.plane()]
    for dy in (1, 2, 3):
        for zt, dev in at.line():
            partners.append(dev + (((at.y + dy) % 4) - at.y) * 8)
    for dev in partners:
        pl.semaphore_signal(barrier, inc=1, device_id=(dev,), device_id_type=MESH)
    pl.semaphore_wait(barrier, len(partners))


def scan(at, links, state, out, sib, mine_c, zbuf, pbuf, ret, ebuf, give, reverse):
    mine, other = rows(at.c * 256, 256), rows((1 - at.c) * 256, 256)
    first = links.start(state.at[other], sib, at.sibling)
    yield
    arrived([first])
    chip = state[mine, :] + sib[...]
    for k in range(4):
        pack(mine_c.at[k], chip[k * 64 : (k + 1) * 64])
    copies = []
    for zt, dev in at.line():
        copies.append(links.start(mine_c.at[zt], zbuf.at[at.z], dev))
    zbuf[at.z] = mine_c[at.z]
    yield
    arrived(copies)
    parts = [unpack(zbuf.at[k]) for k in range(4)]
    pack(pbuf.at[at.g], parts[0] + parts[1] + parts[2] + parts[3])
    copies = []
    for dx, dy in PLANE:
        gt = ((at.x + dx) % 4) * 4 + (at.y + dy) % 4
        gs = ((at.x + 4 - dx) % 4) * 4 + (at.y + 4 - dy) % 4
        goes, comes = (gt < at.g, gs > at.g) if reverse else (gt > at.g, gs < at.g)
        copies.append((comes, links.start(pbuf.at[at.g], pbuf.at[at.g], gt * 8 + at.me % 8, goes)))
    yield
    for comes, copy in copies:
        pl.when(comes)(copy.wait_recv)
    total = jnp.zeros((64, HS), F32)
    for k in range(16):
        passed = (k > at.g) if reverse else (k < at.g)
        total = total + jnp.where(passed, unpack(pbuf.at[k]), 0.0)
    for k in range(3, -1, -1) if reverse else range(4):
        pack(ret.at[k], total)
        total = total + parts[k]
    copies = []
    for zt, dev in at.line():
        copies.append(links.start(ret.at[zt], ebuf.at[at.z], dev))
    ebuf[at.z] = ret[at.z]
    yield
    arrived(copies)
    first_core = at.c == (1 if reverse else 0)
    before = jnp.concatenate([unpack(ebuf.at[k]) for k in range(4)], axis=0)
    give[...] = before + jnp.where(first_core, state[mine, :], 0.0)
    last = links.start(give, out.at[mine], at.sibling)
    out[mine, :] = before + jnp.where(first_core, 0.0, sib[...])
    yield
    arrived([last])


def pack(ref, value):
    codes, exponents = code_of([value])
    ref[pl.ds(0, 64), :] = codes[0]
    ref[pl.ds(64, 16), :] = to_i16(jnp.broadcast_to(exponents[0], (16, 128)))


def unpack(ref):
    return number(ref[pl.ds(0, 64), :]) * powers(ref[pl.ds(64, 16), :])[:1]


def code_of(blocks):
    codes, exponents = [], []
    for value in blocks:
        most = jnp.max(jnp.abs(value), axis=0, keepdims=True)
        exponent = jnp.floor(jnp.log2(jnp.maximum(most, 1e-30))) + 1.0
        codes.append(jnp.round(value * jnp.exp2(14.0 - exponent)).astype(jnp.int32).astype(jnp.int16))
        exponents.append(exponent)
    return codes, exponents


def powers(tile):
    return jnp.exp2(tile.astype(jnp.int32).astype(F32) - 14.0)


def number(code):
    return code.astype(jnp.int32).astype(F32)


def to_i16(value):
    return value.astype(jnp.int32).astype(jnp.int16)


def reduce_all(at, links, src, r0, own, r1, zb, r2, pb, ag, pa, full):
    order = [(at.l + d) % 4 for d in (1, 2, 3, 0)]
    copies = []
    for d in (1, 2, 3, 0):
        k = (at.l_sibling + d) % 4
        copies.append(links.start(src.at[rows((1 - at.c) * 256 + k * 64, 64)], r0.at[k], at.sibling))
    yield
    line = []
    pad = jnp.zeros((8, 128), F32)
    for i, (lt, dev) in enumerate(at.sum_line()):
        arrived([copies[i]])
        blocks = [
            src[rows(at.c * 256 + lt * 64, 64), pl.ds(j * 128, 128)] + r0[lt, :, pl.ds(j * 128, 128)] for j in range(8)
        ]
        codes, exponents = code_of(blocks)
        for j in range(8):
            r1[i, pl.ds(j * 64, 64), :] = codes[j]
        r1[i, pl.ds(512, 16), :] = to_i16(jnp.concatenate(exponents + [pad], axis=0))
        line.append(links.start(r1.at[i], zb.at[i], dev))
    arrived([copies[3]])
    for j in range(8):
        own[pl.ds(j * 64, 64), :] = (
            src[rows(at.c * 256 + at.l * 64, 64), pl.ds(j * 128, 128)] + r0[at.l, :, pl.ds(j * 128, 128)]
        )
    yield
    arrived(line)
    scales = [powers(zb[i, pl.ds(512, 16), :]) for i in range(3)]
    pad = jnp.zeros((14, 128), F32)
    for k in range(16):
        pk, qk = k // 4, k % 4
        blocks = []
        for j in (2 * qk, 2 * qk + 1):
            part = pl.ds(j * 64 + pk * 16, 16)
            value = own[part, :]
            for i in range(3):
                value = value + number(zb[i, part, :]) * scales[i][j : j + 1]
            blocks.append(value)
        codes, exponents = code_of(blocks)
        r2[k, pl.ds(0, 16), :] = codes[0]
        r2[k, pl.ds(16, 16), :] = codes[1]
        r2[k, pl.ds(32, 16), :] = to_i16(jnp.concatenate(exponents + [pad], axis=0))
    plane = []
    for i, (k, dev) in enumerate(at.sum_plane()):
        plane.append(links.start(r2.at[k], pb.at[i], dev))
    yield
    arrived(plane)
    scale = powers(r2[at.pq, pl.ds(32, 16), :])
    total = [number(r2[at.pq, pl.ds(16 * b, 16), :]) * scale[b : b + 1] for b in range(2)]
    for i in range(15):
        scale = powers(pb[i, pl.ds(32, 16), :])
        total = [total[b] + number(pb[i, pl.ds(16 * b, 16), :]) * scale[b : b + 1] for b in range(2)]
    codes, exponents = code_of(total)
    row = lax.broadcasted_iota(jnp.int32, (16, 128), 0) - 2 * (at.pq % 8)
    ag[pl.ds(0, 16), :] = codes[0]
    ag[pl.ds(16, 16), :] = codes[1]
    ag[pl.ds(32, 16), :] = to_i16(jnp.where(row == 0, exponents[0], jnp.where(row == 1, exponents[1], 0.0)))
    plane = []
    for k, dev in at.sum_plane():
        plane.append(links.start(ag, pa.at[at.pq], dev))
    pa[at.pq] = ag[...]
    yield
    arrived(plane)
    mine = full.at[at.c, at.l]
    for k in range(16):
        mine[pl.ds(k * 32, 32), :] = pa[k, pl.ds(0, 32), :]
    for b in range(2):
        tile = pa[8 * b, pl.ds(32, 16), :].astype(jnp.int32)
        for k in range(1, 8):
            tile = tile + pa[8 * b + k, pl.ds(32, 16), :].astype(jnp.int32)
        mine[pl.ds(512 + 16 * b, 16), :] = tile.astype(jnp.int16)
    line = []
    for lt, dev in at.sum_line():
        line.append(links.start(mine, mine, dev))
    other = [links.start(mine, mine, at.sibling)]
    yield
    for d in (1, 2, 3):
        arrived([line[d - 1]])
        k = (at.l + 4 - d) % 4
        other.append(links.start(full.at[at.c, k], full.at[at.c, k], at.sibling))
    yield
    arrived(other)


def decode(early, late, small, qkv_out, out_out, head_out, gain_out, sib_out):
    for full, first in ((early, 0), (late, 1024)):
        scales = [powers(full[0, 0, pl.ds(512 + 16 * b, 16), :]) for b in range(2)]
        for g in range(16):
            for b in range(2):
                e = 2 * (g % 8) + b
                value = number(full[0, 0, pl.ds(g * 32 + b * 16, 16), :]) * scales[g // 8][e : e + 1]
                column = first + (g % 4) * 256 + b * 128
                out, column = (out_out, column) if column < D else (qkv_out, column - D)
                out[pl.ds(g // 4 * 16, 16), pl.ds(column, 128)] = value
    head_out[...] = small[pl.ds(0, 8), :]
    gain_out[...] = small[pl.ds(8, 1), :]
    sib_out[...] = small[pl.ds(16, 8), :]


def reduce_small(at, links, xs, xo, x0, x1, xz, xp):
    mine, other = rows(at.c * 16, 16), rows((1 - at.c) * 16, 16)
    first = links.start(xs.at[other], x0, at.sibling)
    yield
    arrived([first])
    total = xs[mine, :] + x0[...]
    for k in range(4):
        x1[k] = total[:, k * 128 : (k + 1) * 128]
    copies = []
    for lt, dev in at.sum_line():
        copies.append(links.start(x1.at[lt], xz.at[at.l], dev))
    xz[at.l] = x1[at.l]
    yield
    arrived(copies)
    xp[at.pq] = xz[0] + xz[1] + xz[2] + xz[3]
    copies = []
    for k, dev in at.sum_plane():
        copies.append(links.start(xp.at[at.pq], xp.at[at.pq], dev))
    yield
    arrived(copies)
    total = xp[0]
    for k in range(1, 16):
        total = total + xp[k]
    place = xo.at[mine, rows(at.l * 128, 128)]
    place[...] = total
    copies = []
    for lt, dev in at.sum_line():
        copies.append(links.start(place, place, dev))
    yield
    arrived(copies)
    last = links.start(xo.at[mine], xo.at[mine], at.sibling)
    yield
    arrived([last])


def step(generator):
    for _ in generator:
        return True
    return False


def finish(generator):
    while step(generator):
        pass


def head(h, part=0):
    return pl.ds(part * D + h * HS, HS)


def block(b):
    return pl.ds(b * RB, RB)


def lower(b):
    row = lax.broadcasted_iota(jnp.int32, (RB, (b + 1) * RB), 0) + b * RB
    col = lax.broadcasted_iota(jnp.int32, (RB, (b + 1) * RB), 1)
    return col <= row


def kernel(
    parents, counts_in, occupancy_in, sib_in, gain_in, w_qkv_in, w_out_in, w_head_in,
    e_full, l_full, small_out,
    window, ends, offz, offp, offs, inputs, inv_in, normed, packed, onehot,
    scores, numer, resid, inv_out, final, attended, d_logits, d_resid, d_resid_b, wide, grads, d_packed,
    d_local, states, prefix, qstates, suffix,
    f_sib, f_chip, f_z, f_p, f_ret, f_e, f_give,
    b_sib, b_chip, b_z, b_p, b_ret, b_e, b_give,
    early, e_r0, e_own, e_r1, e_z, e_r2, e_p, e_ag, e_pa,
    late, l_r0, l_own, l_r1, l_z, l_r2, l_p, l_ag, l_pa,
    small, x0, x1, xz, xp,
    counts, occupancy, sib_table, gain, w_qkv, w_out, w_head,
    send, recv, load,
):
    at = Place()
    links = Links(send, recv)
    own = pl.ds(PAR, PAR)
    pairs = [
        (counts_in, counts), (parents, window.at[own]), (sib_in, sib_table), (gain_in, gain), (w_qkv_in, w_qkv),
        (occupancy_in, occupancy), (w_out_in, w_out), (w_head_in, w_head),
    ]
    loads = [pltpu.make_async_copy(src, dst, load.at[i]) for i, (src, dst) in enumerate(pairs)]
    for copy in loads:
        copy.start()
    greet(at)

    loads[0].wait()
    count = jnp.broadcast_to(counts[...].astype(F32), (16, PAR))
    whole = jnp.sum(count[:8], axis=1, keepdims=True)
    offs[0] = jnp.broadcast_to(whole, (8, 128))
    first = links.start(offs.at[0], offs.at[1], at.sibling)
    tri = (
        lax.broadcasted_iota(jnp.int32, (PAR, PAR), 0) <= lax.broadcasted_iota(jnp.int32, (PAR, PAR), 1)
    ).astype(BF16)
    local_ends = dot(count.astype(BF16), tri)[:8]
    ends[1, :8] = local_ends
    ends[1, 8:] = count[:8]
    arrived([first])
    offset = jnp.where(at.c == 1, offs[1], 0.0)
    offz[at.z] = offs[0] + offs[1]
    copies = [links.start(offz.at[at.z], offz.at[at.z], dev) for zt, dev in at.line()]
    halo = [
        links.start(ends.at[1], ends.at[0], at.next),
        links.start(ends.at[1], ends.at[2], at.prev),
        links.start(parents, window.at[pl.ds(0, PAR)], at.next),
        links.start(parents, window.at[pl.ds(2 * PAR, PAR)], at.prev),
    ]
    arrived(copies)
    offp[at.g] = offz[0] + offz[1] + offz[2] + offz[3]
    copies = [links.start(offp.at[at.g], offp.at[at.g], dev) for xt, yt, dev in at.plane()]
    for k in range(4):
        offset = offset + jnp.where(k < at.z, offz[k], 0.0)
    arrived(copies)
    for k in range(16):
        offset = offset + jnp.where(k < at.g, offp[k], 0.0)
    shift = (at.me * N).astype(F32) - offset[:1, :1]

    arrived(halo)
    for copy in loads[1:]:
        copy.wait()
    own_total = whole[:1, :1]
    low_total = ends[0, :1, PAR - 1 :]
    end_row = jnp.concatenate([ends[0, :1] - low_total, local_ends[:1], ends[2, :1] + own_total], axis=1)
    count_row = jnp.concatenate([ends[0, 8:9], count[:1], ends[2, 8:9]], axis=1)
    start_row = end_row - count_row
    lanes8 = lax.broadcasted_iota(jnp.int32, (128, 8), 0)
    spread = (lanes8 == lax.broadcasted_iota(jnp.int32, (128, 8), 1) + 16).astype(BF16)
    sib_rows = dot(spread, sib_table[...]).astype(BF16)
    lane = lax.broadcasted_iota(jnp.int32, (RB, 128), 1)
    for b in range(BLOCKS):
        place = lax.broadcasted_iota(jnp.int32, (RB, 1), 0).astype(F32) + (shift + float(b * RB))
        child = (start_row <= place) & (place < end_row)
        chosen = jnp.where(child, 1.0, 0.0).astype(BF16)
        start_of = jnp.sum(jnp.where(child, start_row, 0.0), axis=1, keepdims=True)
        rank = (place - start_of).astype(jnp.int32)
        hot = (rank + 16 == lane).astype(F32).astype(BF16)
        onehot[block(b), :] = hot
        value = (dot(chosen, window[...]) + dot(hot, sib_rows)).astype(BF16)
        inputs[block(b), :] = value
        value = value.astype(F32)
        inverse = lax.rsqrt(jnp.mean(value * value, axis=-1, keepdims=True) + 1e-06)
        inv_in[block(b), :] = inverse
        normed[block(b), :] = (value * inverse * gain[...]).astype(BF16)
    packed[...] = dot(normed[...], w_qkv[...]).astype(BF16)
    for h in range(HEADS):
        states[pl.ds(h * HS, HS), :] = dot_tn(packed[:, head(h, 1)], packed[:, head(h, 2)])

    forward = scan(at, links, states, prefix, f_sib, f_chip, f_z, f_p, f_ret, f_e, f_give, False)
    step(forward)
    for h in range(HEADS):
        for b in range(BLOCKS):
            keys, values = packed[: (b + 1) * RB, head(h, 1)], packed[: (b + 1) * RB, head(h, 2)]
            score = jnp.where(lower(b), dot_nt(packed[block(b), head(h)], keys), 0.0).astype(BF16)
            scores[h, block(b), : (b + 1) * RB] = score
            numer[block(b), head(h)] = dot(score, values)
        step(forward)
    finish(forward)

    for h in range(HEADS):
        high, low = split(prefix[pl.ds(h * HS, HS), :])
        q = packed[:, head(h)]
        wide[:, head(h)] = dot(q, high) + dot(q, low)
    scale = float(DEVS * N) ** (-0.5)
    lane8 = lax.broadcasted_iota(jnp.int32, (RB, 8), 1)
    symbols = jnp.broadcast_to(occupancy[...].astype(F32), (8, N)).T.astype(jnp.int32)
    inv_heads = []
    for b in range(BLOCKS):
        for h in range(HEADS):
            value = numer[block(b), head(h)] + wide[block(b), head(h)]
            numer[block(b), head(h)] = value
            inverse = lax.rsqrt(jnp.mean(value * value, axis=-1, keepdims=True) + 1e-05)
            attended[block(b), head(h)] = (value * inverse).astype(BF16)
            inv_heads.append(inverse)
    wide[...] = dot(attended[...], w_out[...])
    for b in range(BLOCKS):
        value = inputs[block(b), :].astype(F32) + wide[block(b), :]
        resid[block(b), :] = value
        inverse = lax.rsqrt(jnp.mean(value * value, axis=-1, keepdims=True) + 1e-06)
        inv_out[block(b), :] = inverse
        last = (value * inverse).astype(BF16)
        final[block(b), :] = last
        logits = dot_nt(last, w_head[...])
        target = ((symbols[b * RB : (b + 1) * RB] >> lane8) & 1).astype(F32)
        small_grad = ((jax.nn.sigmoid(logits) - target) * scale).astype(BF16)
        d_logits[block(b), :] = small_grad
        d_final = dot(small_grad, w_head[...])
        mean = jnp.mean(d_final * value, axis=-1, keepdims=True)
        d_value = inverse * d_final - value * (inverse * inverse * inverse) * mean
        d_resid[block(b), :] = d_value
        d_resid_b[block(b), :] = d_value.astype(BF16)
    wide[...] = dot_nt(d_resid_b[...], w_out[...])
    for b in range(BLOCKS):
        for h in range(HEADS):
            piece, value, inverse = wide[block(b), head(h)], numer[block(b), head(h)], inv_heads[b * HEADS + h]
            mean = jnp.mean(piece * value, axis=-1, keepdims=True)
            grads[block(b), head(h)] = (inverse * piece - value * (inverse * inverse * inverse) * mean).astype(BF16)
    for h in range(HEADS):
        qstates[pl.ds(h * HS, HS), :] = dot_tn(packed[:, head(h)], grads[:, head(h)])

    backward = scan(at, links, qstates, suffix, b_sib, b_chip, b_z, b_p, b_ret, b_e, b_give, True)
    step(backward)
    early[:, pl.ds(0, D)] = dot_tn(attended[...], d_resid_b[...])
    step(backward)
    for h in range(HEADS):
        high, low = split(prefix[pl.ds(h * HS, HS), :])
        g = grads[:, head(h)]
        wide[:, head(h)] = dot_nt(g, high) + dot_nt(g, low)
    d_local[...] = jnp.zeros_like(d_local)
    for h in range(HEADS):
        for b in range(BLOCKS):
            upto = pl.ds(0, (b + 1) * RB)
            g, q = grads[block(b), head(h)], packed[block(b), head(h)]
            back = jnp.where(lower(b), dot_nt(g, packed[upto, head(h, 2)]), 0.0).astype(BF16)
            dq = dot(back, packed[upto, head(h, 1)]) + wide[block(b), head(h)]
            d_packed[block(b), head(h)] = dq.astype(BF16)
            d_local[upto, head(h)] += dot_tn(back, q)
            d_local[upto, head(h, 1)] += dot_tn(scores[h, block(b), upto], g)
        if h == 1:
            step(backward)
    step(backward)
    early[:, pl.ds(D, D)] = dot_tn(normed[...], d_packed[:, pl.ds(0, D)])
    early_sum = reduce_all(at, links, early, e_r0, e_own, e_r1, e_z, e_r2, e_p, e_ag, e_pa, e_full)
    step(early_sum)
    wide[...] = dot_nt(d_packed[:, pl.ds(0, D)], w_qkv[:, pl.ds(0, D)])
    step(backward)
    step(early_sum)
    finish(backward)

    for h in range(HEADS):
        high, low = split(suffix[pl.ds(h * HS, HS), :])
        k, v = packed[:, head(h, 1)], packed[:, head(h, 2)]
        d_packed[:, head(h, 1)] = (d_local[:, head(h)] + dot_nt(v, high) + dot_nt(v, low)).astype(BF16)
        d_packed[:, head(h, 2)] = (d_local[:, head(h, 1)] + dot(k, high) + dot(k, low)).astype(BF16)
    late[...] = dot_tn(normed[...], d_packed[:, pl.ds(D, 2 * D)])
    late_sum = reduce_all(at, links, late, l_r0, l_own, l_r1, l_z, l_r2, l_p, l_ag, l_pa, l_full)
    step(late_sum)
    step(early_sum)
    step(late_sum)
    wide[...] += dot_nt(d_packed[:, pl.ds(D, 2 * D)], w_qkv[:, pl.ds(D, 2 * D)])
    grad_gain = jnp.zeros((1, D), F32)
    grad_sib = jnp.zeros((128, D), F32)
    for b in range(BLOCKS):
        value, inverse, slope = inputs[block(b), :].astype(F32), inv_in[block(b), :], wide[block(b), :]
        grad_gain = grad_gain + jnp.sum(slope * value * inverse, axis=0, keepdims=True)
        scaled = slope * gain[...]
        mean = jnp.mean(scaled * value, axis=-1, keepdims=True)
        d_in = inverse * scaled - value * (inverse * inverse * inverse) * mean + d_resid[block(b), :]
        high, low = split(d_in)
        grad_sib = grad_sib + dot_tn(onehot[block(b), :], high) + dot_tn(onehot[block(b), :], low)
    small[pl.ds(0, 8), :] = dot_tn(d_logits[...], final[...])
    small[pl.ds(8, 8), :] = jnp.broadcast_to(grad_gain, (8, D))
    small[pl.ds(16, 16), :] = grad_sib[16:32]
    small_sum = reduce_small(at, links, small, small_out, x0, x1, xz, xp)
    step(small_sum)
    step(early_sum)
    more = True
    while more:
        step(small_sum)
        more = step(late_sum)
        step(early_sum)
    finish(early_sum)
    finish(small_sum)
    links.finish()


def vm(shape, dtype=F32):
    return pltpu.VMEM(shape, dtype)


def scan_buffers():
    coded = [vm((k, 80, 128), jnp.int16) for k in (4, 4, 16, 4, 4)]
    return [vm((256, HS)), *coded, vm((256, HS))]


def sum_buffers():
    i16 = jnp.int16
    return [
        vm((N, 1024)), vm((4, 64, 1024)), vm((512, 128)), vm((3, 528, 128), i16), vm((3, 528, 128), i16),
        vm((16, 48, 128), i16), vm((15, 48, 128), i16), vm((48, 128), i16), vm((16, 48, 128), i16),
    ]


def shards(parent_rows, counts, occupancy, sib_table, gain, w_qkv, w_out, w_head):
    scratch = [
        vm((3 * PAR, D), BF16), vm((3, 16, PAR)), vm((4, 8, 128)), vm((16, 8, 128)), vm((2, 8, 128)),
        vm((N, D), BF16), vm((N, 1)), vm((N, D), BF16), vm((N, 3 * D), BF16), vm((N, 128), BF16),
        vm((HEADS, N, N), BF16), vm((N, D)), vm((N, D)), vm((N, 1)), vm((N, D), BF16), vm((N, D), BF16),
        vm((N, 8), BF16), vm((N, D)), vm((N, D), BF16), vm((N, D)), vm((N, D), BF16), vm((N, 3 * D), BF16),
        vm((N, 2 * D)), vm((N, HS)), vm((N, HS)), vm((N, HS)), vm((N, HS)),
        *scan_buffers(), *scan_buffers(), *sum_buffers(), *sum_buffers(),
        vm((32, D)), vm((16, D)), vm((4, 16, 128)), vm((4, 16, 128)), vm((16, 16, 128)),
        vm((1, PAR), jnp.int32), vm((1, N), jnp.int32), vm((8, D), BF16), vm((1, D)), vm((D, 3 * D), BF16), vm((D, D), BF16),
        vm((8, D), BF16),
        pltpu.SemaphoreType.DMA((COPIES,)), pltpu.SemaphoreType.DMA((COPIES,)), pltpu.SemaphoreType.DMA((8,)),
    ]
    spec = pl.BlockSpec(memory_space=pltpu.VMEM)
    codes = jax.ShapeDtypeStruct((2, 4, 544, 128), jnp.int16)
    early, late, small = pl.pallas_call(
        kernel,
        out_shape=[codes, codes, jax.ShapeDtypeStruct((32, D), F32)],
        in_specs=[pl.BlockSpec(memory_space=pltpu.HBM)] * 8,
        out_specs=[spec] * 3,
        scratch_shapes=scratch,
        compiler_params=pltpu.CompilerParams(
            collective_id=0, has_side_effects=True, vmem_limit_bytes=58 * 1024 * 1024
        ),
        name="train_step",
    )(
        parent_rows, counts.reshape(1, PAR), occupancy.reshape(1, N), sib_table, gain.reshape(1, D),
        w_qkv, w_out, w_head.T,
    )
    piece = pl.BlockSpec((1, 1, 544, 128), lambda i: (i // 4, i % 4, 0, 0))
    whole = [(8, D), (1, D), (8, D)]
    grad_qkv, grad_out, grad_head, grad_gain, grad_sib = pl.pallas_call(
        decode,
        grid=(8,),
        in_specs=[piece, piece, pl.BlockSpec((32, D), lambda i: (0, 0))],
        out_specs=[
            pl.BlockSpec((64, 3 * D), lambda i: (i, 0)),
            pl.BlockSpec((64, D), lambda i: (i, 0)),
            *[pl.BlockSpec(shape, lambda i: (0, 0)) for shape in whole],
        ],
        out_shape=[jax.ShapeDtypeStruct(shape, F32) for shape in [(D, 3 * D), (D, D), *whole]],
        name="decode",
    )(early, late, small)
    return grad_qkv, grad_out, grad_head.T, grad_gain.reshape(D), grad_sib


def solution(mesh):
    placed = (P("seq", None), P("seq"), P("seq"), P(), P(), P(), P(), P())
    return jax.shard_map(
        shards, mesh=mesh, in_specs=placed, out_specs=(P(), P(), P(), P(), P()), check_vma=False
    )
```

```python
import jax
import jax.numpy as jnp
from jax import lax
from jax.experimental import pallas as pl
from jax.experimental.pallas import tpu as pltpu
from jax.sharding import PartitionSpec as P

MESH = pl.DeviceIdType.MESH
F32, BF16 = jnp.float32, jnp.bfloat16
HEADS, HS, D = 4, 128, 512
N, PAR, DEVS = 512, 256, 128
RB = 128
BLOCKS = N // RB
COPIES = 184
PLANE = [(dx, dy) for dx in range(4) for dy in range(4) if dx or dy]


def dot(a, b):
    return jnp.dot(a, b, preferred_element_type=F32)


def dot_tn(a, b):
    return lax.dot_general(a, b, (((0,), (0,)), ((), ())), preferred_element_type=F32)


def dot_nt(a, b):
    return lax.dot_general(a, b, (((1,), (1,)), ((), ())), preferred_element_type=F32)


def split(value):
    high = value.astype(BF16)
    return high, (value - high.astype(F32)).astype(BF16)


def rows(start, count):
    return pl.ds(pl.multiple_of(start, count), count)


class Place:
    def __init__(self):
        me = lax.axis_index("seq")
        self.me = me
        self.x, self.y, self.z, self.c = me // 32, (me // 8) % 4, (me // 2) % 4, me % 2
        self.g = self.x * 4 + self.y
        self.sibling = me + 1 - 2 * self.c
        c = self.c
        self.l, self.l_step = self.z + c * (self.x - self.z), 2 + 30 * c
        self.p, self.p_step = self.x + c * (self.y - self.x), 32 - 24 * c
        self.q, self.q_step = self.y + c * (self.z - self.y), 8 - 6 * c
        self.l_sibling = self.x + c * (self.z - self.x)
        self.pq = self.p * 4 + self.q
        self.next = (me + 1) % DEVS
        self.prev = (me + DEVS - 1) % DEVS

    def line(self):
        for d in (1, 2, 3):
            zt = (self.z + d) % 4
            yield zt, self.me - 2 * self.z + 2 * zt

    def plane(self):
        for dx, dy in PLANE:
            xt, yt = (self.x + dx) % 4, (self.y + dy) % 4
            yield xt, yt, (xt * 4 + yt) * 8 + self.me % 8


    def sum_line(self):
        for d in (1, 2, 3):
            lt = (self.l + d) % 4
            yield lt, self.me + (lt - self.l) * self.l_step

    def sum_plane(self):
        for dp, dq in PLANE:
            pt, qt = (self.p + dp) % 4, (self.q + dq) % 4
            yield pt * 4 + qt, self.me + (pt - self.p) * self.p_step + (qt - self.q) * self.q_step


class Links:
    def __init__(self, send, recv):
        self.send, self.recv, self.sent = send, recv, []

    def start(self, src, dst, device, when=None):
        k = len(self.sent)
        copy = pltpu.make_async_remote_copy(
            src_ref=src,
            dst_ref=dst,
            send_sem=self.send.at[k],
            recv_sem=self.recv.at[k],
            device_id=(device,),
            device_id_type=MESH,
        )
        if when is None:
            copy.start()
        else:
            pl.when(when)(copy.start)
        self.sent.append((copy, when))
        return copy

    def finish(self):
        for copy, when in self.sent:
            if when is None:
                copy.wait_send()
            else:
                pl.when(when)(copy.wait_send)


def arrived(copies):
    for copy in copies:
        copy.wait_recv()


def greet(at):
    barrier = pltpu.get_barrier_semaphore()
    far = at.me + DEVS - 1 + 2 * at.c
    partners = [at.sibling, far % DEVS]
    partners += [dev for zt, dev in at.line()] + [dev for xt, yt, dev in at.plane()]
    for dy in (1, 2, 3):
        for zt, dev in at.line():
            partners.append(dev + (((at.y + dy) % 4) - at.y) * 8)
    for dev in partners:
        pl.semaphore_signal(barrier, inc=1, device_id=(dev,), device_id_type=MESH)
    return lambda: pl.semaphore_wait(barrier, len(partners))


def scan(at, links, state, out, sib, mine_c, zbuf, pbuf, ret, ebuf, give, reverse):
    mine, other = rows(at.c * 256, 256), rows((1 - at.c) * 256, 256)
    first = links.start(state.at[other], sib, at.sibling)
    yield
    arrived([first])
    chip = state[mine, :] + sib[...]
    for k in range(4):
        pack(mine_c.at[k], chip[k * 64 : (k + 1) * 64])
    copies = []
    for zt, dev in at.line():
        copies.append(links.start(mine_c.at[zt], zbuf.at[at.z], dev))
    zbuf[at.z] = mine_c[at.z]
    yield
    arrived(copies)
    parts = [unpack(zbuf.at[k]) for k in range(4)]
    pack(pbuf.at[at.g], parts[0] + parts[1] + parts[2] + parts[3])
    copies = []
    for dx, dy in PLANE:
        gt = ((at.x + dx) % 4) * 4 + (at.y + dy) % 4
        gs = ((at.x + 4 - dx) % 4) * 4 + (at.y + 4 - dy) % 4
        goes, comes = (gt < at.g, gs > at.g) if reverse else (gt > at.g, gs < at.g)
        copies.append((comes, links.start(pbuf.at[at.g], pbuf.at[at.g], gt * 8 + at.me % 8, goes)))
    yield
    for comes, copy in copies:
        pl.when(comes)(copy.wait_recv)
    total = jnp.zeros((64, HS), F32)
    for k in range(16):
        passed = (k > at.g) if reverse else (k < at.g)
        total = total + jnp.where(passed, unpack(pbuf.at[k]), 0.0)
    for k in range(3, -1, -1) if reverse else range(4):
        pack(ret.at[k], total)
        total = total + parts[k]
    copies = []
    for zt, dev in at.line():
        copies.append(links.start(ret.at[zt], ebuf.at[at.z], dev))
    ebuf[at.z] = ret[at.z]
    yield
    arrived(copies)
    first_core = at.c == (1 if reverse else 0)
    before = jnp.concatenate([unpack(ebuf.at[k]) for k in range(4)], axis=0)
    give[...] = before + jnp.where(first_core, state[mine, :], 0.0)
    last = links.start(give, out.at[mine], at.sibling)
    out[mine, :] = before + jnp.where(first_core, 0.0, sib[...])
    yield
    arrived([last])


def pack(ref, value):
    codes, exponents = code_of([value])
    ref[pl.ds(0, 64), :] = codes[0]
    ref[pl.ds(64, 16), :] = to_i16(jnp.broadcast_to(exponents[0], (16, 128)))


def unpack(ref):
    return number(ref[pl.ds(0, 64), :]) * powers(ref[pl.ds(64, 16), :])[:1]


def code_of(blocks):
    codes, exponents = [], []
    for value in blocks:
        most = jnp.max(jnp.abs(value), axis=0, keepdims=True)
        exponent = jnp.floor(jnp.log2(jnp.maximum(most, 1e-30))) + 1.0
        codes.append(jnp.round(value * jnp.exp2(14.0 - exponent)).astype(jnp.int32).astype(jnp.int16))
        exponents.append(exponent)
    return codes, exponents


def powers(tile):
    return jnp.exp2(tile.astype(jnp.int32).astype(F32) - 14.0)


def number(code):
    return code.astype(jnp.int32).astype(F32)


def to_i16(value):
    return value.astype(jnp.int32).astype(jnp.int16)


def reduce_all(at, links, src, r0, own, r1, zb, r2, pb, ag, pa, full):
    order = [(at.l + d) % 4 for d in (1, 2, 3, 0)]
    copies = []
    for d in (1, 2, 3, 0):
        k = (at.l_sibling + d) % 4
        copies.append(links.start(src.at[rows((1 - at.c) * 256 + k * 64, 64)], r0.at[k], at.sibling))
    yield
    line = []
    pad = jnp.zeros((8, 128), F32)
    for i, (lt, dev) in enumerate(at.sum_line()):
        arrived([copies[i]])
        blocks = [
            src[rows(at.c * 256 + lt * 64, 64), pl.ds(j * 128, 128)] + r0[lt, :, pl.ds(j * 128, 128)] for j in range(8)
        ]
        codes, exponents = code_of(blocks)
        for j in range(8):
            r1[i, pl.ds(j * 64, 64), :] = codes[j]
        r1[i, pl.ds(512, 16), :] = to_i16(jnp.concatenate(exponents + [pad], axis=0))
        line.append(links.start(r1.at[i], zb.at[i], dev))
    arrived([copies[3]])
    for j in range(8):
        own[pl.ds(j * 64, 64), :] = (
            src[rows(at.c * 256 + at.l * 64, 64), pl.ds(j * 128, 128)] + r0[at.l, :, pl.ds(j * 128, 128)]
        )
    yield
    arrived(line)
    scales = [powers(zb[i, pl.ds(512, 16), :]) for i in range(3)]
    pad = jnp.zeros((14, 128), F32)
    for k in range(16):
        pk, qk = k // 4, k % 4
        blocks = []
        for j in (2 * qk, 2 * qk + 1):
            part = pl.ds(j * 64 + pk * 16, 16)
            value = own[part, :]
            for i in range(3):
                value = value + number(zb[i, part, :]) * scales[i][j : j + 1]
            blocks.append(value)
        codes, exponents = code_of(blocks)
        r2[k, pl.ds(0, 16), :] = codes[0]
        r2[k, pl.ds(16, 16), :] = codes[1]
        r2[k, pl.ds(32, 16), :] = to_i16(jnp.concatenate(exponents + [pad], axis=0))
    plane = []
    for i, (k, dev) in enumerate(at.sum_plane()):
        plane.append(links.start(r2.at[k], pb.at[i], dev))
    yield
    arrived(plane)
    scale = powers(r2[at.pq, pl.ds(32, 16), :])
    total = [number(r2[at.pq, pl.ds(16 * b, 16), :]) * scale[b : b + 1] for b in range(2)]
    for i in range(15):
        scale = powers(pb[i, pl.ds(32, 16), :])
        total = [total[b] + number(pb[i, pl.ds(16 * b, 16), :]) * scale[b : b + 1] for b in range(2)]
    codes, exponents = code_of(total)
    row = lax.broadcasted_iota(jnp.int32, (16, 128), 0) - 2 * (at.pq % 8)
    ag[pl.ds(0, 16), :] = codes[0]
    ag[pl.ds(16, 16), :] = codes[1]
    ag[pl.ds(32, 16), :] = to_i16(jnp.where(row == 0, exponents[0], jnp.where(row == 1, exponents[1], 0.0)))
    plane = []
    for k, dev in at.sum_plane():
        plane.append(links.start(ag, pa.at[at.pq], dev))
    pa[at.pq] = ag[...]
    yield
    arrived(plane)
    mine = full.at[at.c, at.l]
    for k in range(16):
        mine[pl.ds(k * 32, 32), :] = pa[k, pl.ds(0, 32), :]
    for b in range(2):
        tile = pa[8 * b, pl.ds(32, 16), :].astype(jnp.int32)
        for k in range(1, 8):
            tile = tile + pa[8 * b + k, pl.ds(32, 16), :].astype(jnp.int32)
        mine[pl.ds(512 + 16 * b, 16), :] = tile.astype(jnp.int16)
    line = []
    for lt, dev in at.sum_line():
        line.append(links.start(mine, mine, dev))
    other = [links.start(mine, mine, at.sibling)]
    yield
    for d in (1, 2, 3):
        arrived([line[d - 1]])
        k = (at.l + 4 - d) % 4
        other.append(links.start(full.at[at.c, k], full.at[at.c, k], at.sibling))
    yield
    arrived(other)


def decode(early_in, late_in, small, qkv_out, out_out, head_out, gain_out, sib_out, early, late, qkv, out, load, store):
    loads, stores = [], []
    for k in range(8):
        for i, (src, dst) in enumerate(((early_in, early), (late_in, late))):
            loads.append(pltpu.make_async_copy(src.at[k // 4, k % 4], dst.at[k], load.at[2 * k + i]))
            loads[-1].start()
    for k in range(8):
        for i, (full, first) in enumerate(((early, 0), (late, 1024))):
            loads[2 * k + i].wait()
            scales = [powers(full[k, pl.ds(512 + 16 * b, 16), :]) for b in range(2)]
            for g in range(16):
                for b in range(2):
                    e = 2 * (g % 8) + b
                    value = number(full[k, pl.ds(g * 32 + b * 16, 16), :]) * scales[g // 8][e : e + 1]
                    column = first + (g % 4) * 256 + b * 128
                    to, column = (out, column) if column < D else (qkv, column - D)
                    to[pl.ds(k * 64 + g // 4 * 16, 16), pl.ds(column, 128)] = value
        part = pl.ds(k * 64, 64)
        for i, (src, dst) in enumerate(((qkv, qkv_out), (out, out_out))):
            stores.append(pltpu.make_async_copy(src.at[part], dst.at[part], store.at[2 * k + i]))
            stores[-1].start()
    head_out[...] = small[pl.ds(0, 8), :]
    gain_out[...] = small[pl.ds(8, 1), :]
    sib_out[...] = small[pl.ds(16, 8), :]
    for copy in stores:
        copy.wait()


def reduce_small(at, links, xs, xo, x0, x1, xz, xp):
    mine, other = rows(at.c * 16, 16), rows((1 - at.c) * 16, 16)
    first = links.start(xs.at[other], x0, at.sibling)
    yield
    arrived([first])
    total = xs[mine, :] + x0[...]
    for k in range(4):
        x1[k] = total[:, k * 128 : (k + 1) * 128]
    copies = []
    for lt, dev in at.sum_line():
        copies.append(links.start(x1.at[lt], xz.at[at.l], dev))
    xz[at.l] = x1[at.l]
    yield
    arrived(copies)
    xp[at.pq] = xz[0] + xz[1] + xz[2] + xz[3]
    copies = []
    for k, dev in at.sum_plane():
        copies.append(links.start(xp.at[at.pq], xp.at[at.pq], dev))
    yield
    arrived(copies)
    total = xp[0]
    for k in range(1, 16):
        total = total + xp[k]
    place = xo.at[mine, rows(at.l * 128, 128)]
    place[...] = total
    copies = []
    for lt, dev in at.sum_line():
        copies.append(links.start(place, place, dev))
    yield
    arrived(copies)
    last = links.start(xo.at[mine], xo.at[mine], at.sibling)
    yield
    arrived([last])


def step(generator):
    for _ in generator:
        return True
    return False


def finish(generator):
    while step(generator):
        pass


def head(h, part=0):
    return pl.ds(part * D + h * HS, HS)


def block(b):
    return pl.ds(b * RB, RB)


def lower(b):
    row = lax.broadcasted_iota(jnp.int32, (RB, (b + 1) * RB), 0) + b * RB
    col = lax.broadcasted_iota(jnp.int32, (RB, (b + 1) * RB), 1)
    return col <= row


def kernel(
    parents, counts_in, occupancy_in, sib_in, gain_in, w_qkv_in, w_out_in, w_head_in,
    e_full, l_full, small_out,
    window, ends, offz, offp, offs, inputs, inv_in, normed, packed, onehot,
    scores, numer, resid, inv_out, final, attended, d_logits, d_resid, d_resid_b, wide, grads, d_packed,
    d_local, states, prefix, qstates, suffix,
    f_sib, f_chip, f_z, f_p, f_ret, f_e, f_give,
    b_sib, b_chip, b_z, b_p, b_ret, b_e, b_give,
    early, e_r0, e_own, e_r1, e_z, e_r2, e_p, e_ag, e_pa,
    late, l_r0, l_own, l_r1, l_z, l_r2, l_p, l_ag, l_pa,
    small, x0, x1, xz, xp,
    counts, occupancy, sib_table, gain, w_qkv, w_out, w_head, pair_rows, pair_kv, moved,
    send, recv, load,
):
    at = Place()
    links = Links(send, recv)
    own = pl.ds(PAR, PAR)
    pairs = [
        (counts_in, counts), (parents, window.at[own]), (sib_in, sib_table), (gain_in, gain), (w_qkv_in, w_qkv),
        (occupancy_in, occupancy), (w_out_in, w_out), (w_head_in, w_head),
    ]
    loads = [pltpu.make_async_copy(src, dst, load.at[i]) for i, (src, dst) in enumerate(pairs)]
    for copy in loads:
        copy.start()
    all_here = greet(at)

    loads[0].wait()
    count = jnp.broadcast_to(counts[...].astype(F32), (16, PAR))
    whole = jnp.sum(count[:8], axis=1, keepdims=True)
    offs[0] = jnp.broadcast_to(whole, (8, 128))
    tri = (
        lax.broadcasted_iota(jnp.int32, (PAR, PAR), 0) <= lax.broadcasted_iota(jnp.int32, (PAR, PAR), 1)
    ).astype(BF16)
    local_ends = dot(count.astype(BF16), tri)[:8]
    ends[1, :8] = local_ends
    ends[1, 8:] = count[:8]
    count_col = count[:8].T[:, :1]
    start_col = (local_ends - count[:8]).T[:, :1]
    for copy in loads[1:]:
        copy.wait()
    for r in range(8):
        value = (window[own, :].astype(F32) + sib_table[r : r + 1, :].astype(F32)).astype(BF16).astype(F32)
        inverse = lax.rsqrt(jnp.mean(value * value, axis=-1, keepdims=True) + 1e-06)
        inverse = jnp.where(count_col > float(r), inverse, 0.0)
        pair_rows[pl.ds(r * PAR, PAR), :] = (value * inverse * gain[...]).astype(BF16)
    pair_kv[...] = dot(pair_rows[...], w_qkv[:, pl.ds(D, 2 * D)]).astype(BF16)
    for h in range(HEADS):
        states[pl.ds(h * HS, HS), :] = dot_tn(pair_kv[:, head(h)], pair_kv[:, head(h, 1)])
    all_here()

    first = links.start(offs.at[0], offs.at[1], at.sibling)
    forward = scan(at, links, states, prefix, f_sib, f_chip, f_z, f_p, f_ret, f_e, f_give, False)
    step(forward)
    arrived([first])
    offset = jnp.where(at.c == 1, offs[1], 0.0)
    offz[at.z] = offs[0] + offs[1]
    copies = [links.start(offz.at[at.z], offz.at[at.z], dev) for zt, dev in at.line()]
    step(forward)
    halo = [
        links.start(ends.at[1], ends.at[0], at.next),
        links.start(ends.at[1], ends.at[2], at.prev),
        links.start(parents, window.at[pl.ds(0, PAR)], at.next),
        links.start(parents, window.at[pl.ds(2 * PAR, PAR)], at.prev),
    ]
    arrived(copies)
    offp[at.g] = offz[0] + offz[1] + offz[2] + offz[3]
    copies = [links.start(offp.at[at.g], offp.at[at.g], dev) for xt, yt, dev in at.plane()]
    for k in range(4):
        offset = offset + jnp.where(k < at.z, offz[k], 0.0)
    step(forward)
    arrived(copies)
    for k in range(16):
        offset = offset + jnp.where(k < at.g, offp[k], 0.0)
    shift = (at.me * N).astype(F32) - offset[:1, :1]
    arrived(halo)

    own_total = whole[:1, :1]
    low_total = ends[0, :1, PAR - 1 :]
    end_row = jnp.concatenate([ends[0, :1] - low_total, local_ends[:1], ends[2, :1] + own_total], axis=1)
    count_row = jnp.concatenate([ends[0, 8:9], count[:1], ends[2, 8:9]], axis=1)
    start_row = end_row - count_row
    lanes8 = lax.broadcasted_iota(jnp.int32, (128, 8), 0)
    spread = (lanes8 == lax.broadcasted_iota(jnp.int32, (128, 8), 1) + 16).astype(BF16)
    sib_rows = dot(spread, sib_table[...]).astype(BF16)
    lane = lax.broadcasted_iota(jnp.int32, (RB, 128), 1)
    for b in range(BLOCKS):
        place = lax.broadcasted_iota(jnp.int32, (RB, 1), 0).astype(F32) + (shift + float(b * RB))
        child = (start_row <= place) & (place < end_row)
        chosen = jnp.where(child, 1.0, 0.0).astype(BF16)
        start_of = jnp.sum(jnp.where(child, start_row, 0.0), axis=1, keepdims=True)
        rank = (place - start_of).astype(jnp.int32)
        hot = (rank + 16 == lane).astype(F32).astype(BF16)
        onehot[block(b), :] = hot
        value = (dot(chosen, window[...]) + dot(hot, sib_rows)).astype(BF16)
        inputs[block(b), :] = value
        value = value.astype(F32)
        inverse = lax.rsqrt(jnp.mean(value * value, axis=-1, keepdims=True) + 1e-06)
        inv_in[block(b), :] = inverse
        normed[block(b), :] = (value * inverse * gain[...]).astype(BF16)
    packed[...] = dot(normed[...], w_qkv[...]).astype(BF16)
    step(forward)

    for h in range(HEADS):
        for b in range(BLOCKS):
            keys, values = packed[: (b + 1) * RB, head(h, 1)], packed[: (b + 1) * RB, head(h, 2)]
            score = jnp.where(lower(b), dot_nt(packed[block(b), head(h)], keys), 0.0).astype(BF16)
            scores[h, block(b), : (b + 1) * RB] = score
            numer[block(b), head(h)] = dot(score, values)
        if h == 2:
            step(forward)
    for r in range(8):
        part = pl.ds(r * PAR, PAR)
        before = jnp.where(start_col + float(r) < shift, 1.0, 0.0)
        pair_rows[part, :] = (pair_kv[part, pl.ds(0, D)].astype(F32) * before).astype(BF16)
    place = lax.broadcasted_iota(jnp.int32, (N, 1), 0).astype(F32) + shift
    wide[...] = packed[:, pl.ds(D, D)].astype(F32) * jnp.where(place < 0.0, -1.0, 0.0)
    for h in range(HEADS):
        moved[pl.ds(h * HS, HS), :] = dot_tn(pair_rows[:, head(h)], pair_kv[:, head(h, 1)]) + dot_tn(
            wide[:, head(h)].astype(BF16), packed[:, head(h, 2)]
        )
    finish(forward)
    prefix[...] += moved[...]

    for h in range(HEADS):
        high, low = split(prefix[pl.ds(h * HS, HS), :])
        q = packed[:, head(h)]
        wide[:, head(h)] = dot(q, high) + dot(q, low)
    scale = float(DEVS * N) ** (-0.5)
    lane8 = lax.broadcasted_iota(jnp.int32, (RB, 8), 1)
    symbols = jnp.broadcast_to(occupancy[...].astype(F32), (8, N)).T.astype(jnp.int32)
    inv_heads = []
    for b in range(BLOCKS):
        for h in range(HEADS):
            value = numer[block(b), head(h)] + wide[block(b), head(h)]
            numer[block(b), head(h)] = value
            inverse = lax.rsqrt(jnp.mean(value * value, axis=-1, keepdims=True) + 1e-05)
            attended[block(b), head(h)] = (value * inverse).astype(BF16)
            inv_heads.append(inverse)
    wide[...] = dot(attended[...], w_out[...])
    for b in range(BLOCKS):
        value = inputs[block(b), :].astype(F32) + wide[block(b), :]
        resid[block(b), :] = value
        inverse = lax.rsqrt(jnp.mean(value * value, axis=-1, keepdims=True) + 1e-06)
        inv_out[block(b), :] = inverse
        last = (value * inverse).astype(BF16)
        final[block(b), :] = last
        logits = dot_nt(last, w_head[...])
        target = ((symbols[b * RB : (b + 1) * RB] >> lane8) & 1).astype(F32)
        small_grad = ((jax.nn.sigmoid(logits) - target) * scale).astype(BF16)
        d_logits[block(b), :] = small_grad
        d_final = dot(small_grad, w_head[...])
        mean = jnp.mean(d_final * value, axis=-1, keepdims=True)
        d_value = inverse * d_final - value * (inverse * inverse * inverse) * mean
        d_resid[block(b), :] = d_value
        d_resid_b[block(b), :] = d_value.astype(BF16)
    wide[...] = dot_nt(d_resid_b[...], w_out[...])
    for b in range(BLOCKS):
        for h in range(HEADS):
            piece, value, inverse = wide[block(b), head(h)], numer[block(b), head(h)], inv_heads[b * HEADS + h]
            mean = jnp.mean(piece * value, axis=-1, keepdims=True)
            grads[block(b), head(h)] = (inverse * piece - value * (inverse * inverse * inverse) * mean).astype(BF16)
    for h in range(HEADS):
        qstates[pl.ds(h * HS, HS), :] = dot_tn(packed[:, head(h)], grads[:, head(h)])

    backward = scan(at, links, qstates, suffix, b_sib, b_chip, b_z, b_p, b_ret, b_e, b_give, True)
    step(backward)
    early[:, pl.ds(0, D)] = dot_tn(attended[...], d_resid_b[...])
    step(backward)
    for h in range(HEADS):
        high, low = split(prefix[pl.ds(h * HS, HS), :])
        g = grads[:, head(h)]
        wide[:, head(h)] = dot_nt(g, high) + dot_nt(g, low)
    d_local[...] = jnp.zeros_like(d_local)
    for h in range(HEADS):
        for b in range(BLOCKS):
            upto = pl.ds(0, (b + 1) * RB)
            g, q = grads[block(b), head(h)], packed[block(b), head(h)]
            back = jnp.where(lower(b), dot_nt(g, packed[upto, head(h, 2)]), 0.0).astype(BF16)
            dq = dot(back, packed[upto, head(h, 1)]) + wide[block(b), head(h)]
            d_packed[block(b), head(h)] = dq.astype(BF16)
            d_local[upto, head(h)] += dot_tn(back, q)
            d_local[upto, head(h, 1)] += dot_tn(scores[h, block(b), upto], g)
        if h == 1:
            step(backward)
    step(backward)
    early[:, pl.ds(D, D)] = dot_tn(normed[...], d_packed[:, pl.ds(0, D)])
    early_sum = reduce_all(at, links, early, e_r0, e_own, e_r1, e_z, e_r2, e_p, e_ag, e_pa, e_full)
    step(early_sum)
    wide[...] = dot_nt(d_packed[:, pl.ds(0, D)], w_qkv[:, pl.ds(0, D)])
    step(backward)
    step(early_sum)
    finish(backward)

    for h in range(HEADS):
        high, low = split(suffix[pl.ds(h * HS, HS), :])
        k, v = packed[:, head(h, 1)], packed[:, head(h, 2)]
        d_packed[:, head(h, 1)] = (d_local[:, head(h)] + dot_nt(v, high) + dot_nt(v, low)).astype(BF16)
        d_packed[:, head(h, 2)] = (d_local[:, head(h, 1)] + dot(k, high) + dot(k, low)).astype(BF16)
    late[...] = dot_tn(normed[...], d_packed[:, pl.ds(D, 2 * D)])
    late_sum = reduce_all(at, links, late, l_r0, l_own, l_r1, l_z, l_r2, l_p, l_ag, l_pa, l_full)
    step(late_sum)
    step(early_sum)
    step(late_sum)
    wide[...] += dot_nt(d_packed[:, pl.ds(D, 2 * D)], w_qkv[:, pl.ds(D, 2 * D)])
    grad_gain = jnp.zeros((1, D), F32)
    grad_sib = jnp.zeros((128, D), F32)
    for b in range(BLOCKS):
        value, inverse, slope = inputs[block(b), :].astype(F32), inv_in[block(b), :], wide[block(b), :]
        grad_gain = grad_gain + jnp.sum(slope * value * inverse, axis=0, keepdims=True)
        scaled = slope * gain[...]
        mean = jnp.mean(scaled * value, axis=-1, keepdims=True)
        d_in = inverse * scaled - value * (inverse * inverse * inverse) * mean + d_resid[block(b), :]
        high, low = split(d_in)
        grad_sib = grad_sib + dot_tn(onehot[block(b), :], high) + dot_tn(onehot[block(b), :], low)
    small[pl.ds(0, 8), :] = dot_tn(d_logits[...], final[...])
    small[pl.ds(8, 8), :] = jnp.broadcast_to(grad_gain, (8, D))
    small[pl.ds(16, 16), :] = grad_sib[16:32]
    small_sum = reduce_small(at, links, small, small_out, x0, x1, xz, xp)
    step(small_sum)
    step(early_sum)
    more = True
    while more:
        step(small_sum)
        more = step(late_sum)
        step(early_sum)
    finish(early_sum)
    finish(small_sum)
    links.finish()


def vm(shape, dtype=F32):
    return pltpu.VMEM(shape, dtype)


def scan_buffers():
    coded = [vm((k, 80, 128), jnp.int16) for k in (4, 4, 16, 4, 4)]
    return [vm((256, HS)), *coded, vm((256, HS))]


def sum_buffers():
    i16 = jnp.int16
    return [
        vm((N, 1024)), vm((4, 64, 1024)), vm((512, 128)), vm((3, 528, 128), i16), vm((3, 528, 128), i16),
        vm((16, 48, 128), i16), vm((15, 48, 128), i16), vm((48, 128), i16), vm((16, 48, 128), i16),
    ]


def shards(parent_rows, counts, occupancy, sib_table, gain, w_qkv, w_out, w_head):
    scratch = [
        vm((3 * PAR, D), BF16), vm((3, 16, PAR)), vm((4, 8, 128)), vm((16, 8, 128)), vm((2, 8, 128)),
        vm((N, D), BF16), vm((N, 1)), vm((N, D), BF16), vm((N, 3 * D), BF16), vm((N, 128), BF16),
        vm((HEADS, N, N), BF16), vm((N, D)), vm((N, D)), vm((N, 1)), vm((N, D), BF16), vm((N, D), BF16),
        vm((N, 8), BF16), vm((N, D)), vm((N, D), BF16), vm((N, D)), vm((N, D), BF16), vm((N, 3 * D), BF16),
        vm((N, 2 * D)), vm((N, HS)), vm((N, HS)), vm((N, HS)), vm((N, HS)),
        *scan_buffers(), *scan_buffers(), *sum_buffers(), *sum_buffers(),
        vm((32, D)), vm((16, D)), vm((4, 16, 128)), vm((4, 16, 128)), vm((16, 16, 128)),
        vm((1, PAR), jnp.int32), vm((1, N), jnp.int32), vm((8, D), BF16), vm((1, D)), vm((D, 3 * D), BF16), vm((D, D), BF16),
        vm((8, D), BF16), vm((8 * PAR, D), BF16), vm((8 * PAR, 2 * D), BF16), vm((N, HS)),
        pltpu.SemaphoreType.DMA((COPIES,)), pltpu.SemaphoreType.DMA((COPIES,)), pltpu.SemaphoreType.DMA((8,)),
    ]
    spec = pl.BlockSpec(memory_space=pltpu.VMEM)
    codes = jax.ShapeDtypeStruct((2, 4, 544, 128), jnp.int16)
    early, late, small = pl.pallas_call(
        kernel,
        out_shape=[codes, codes, jax.ShapeDtypeStruct((32, D), F32)],
        in_specs=[pl.BlockSpec(memory_space=pltpu.HBM)] * 8,
        out_specs=[spec] * 3,
        scratch_shapes=scratch,
        compiler_params=pltpu.CompilerParams(
            collective_id=0, has_side_effects=True, vmem_limit_bytes=58 * 1024 * 1024
        ),
        name="train_step",
    )(
        parent_rows, counts.reshape(1, PAR), occupancy.reshape(1, N), sib_table, gain.reshape(1, D),
        w_qkv, w_out, w_head.T,
    )
    hbm = pl.BlockSpec(memory_space=pl.ANY)
    shapes = [(D, 3 * D), (D, D), (8, D), (1, D), (8, D)]
    grad_qkv, grad_out, grad_head, grad_gain, grad_sib = pl.pallas_call(
        decode,
        in_specs=[hbm, hbm, spec],
        out_specs=[hbm, hbm, spec, spec, spec],
        out_shape=[jax.ShapeDtypeStruct(shape, F32) for shape in shapes],
        scratch_shapes=[
            vm((8, 544, 128), jnp.int16), vm((8, 544, 128), jnp.int16), vm((D, 3 * D)), vm((D, D)),
            pltpu.SemaphoreType.DMA((16,)), pltpu.SemaphoreType.DMA((16,)),
        ],
        compiler_params=pltpu.CompilerParams(vmem_limit_bytes=58 * 1024 * 1024),
        name="decode",
    )(early, late, small)
    return grad_qkv, grad_out, grad_head.T, grad_gain.reshape(D), grad_sib


def solution(mesh):
    placed = (P("seq", None), P("seq"), P("seq"), P(), P(), P(), P(), P())
    return jax.shard_map(
        shards, mesh=mesh, in_specs=placed, out_specs=(P(), P(), P(), P(), P()), check_vma=False
    )
```

```python
import jax
import jax.numpy as jnp
from jax import lax
from jax.experimental import pallas as pl
from jax.experimental.pallas import tpu as pltpu
from jax.sharding import PartitionSpec as P

MESH = pl.DeviceIdType.MESH
F32, BF16 = jnp.float32, jnp.bfloat16
HEADS, HS, D = 4, 128, 512
N, PAR, DEVS = 512, 256, 128
RB = 128
BLOCKS = N // RB
COPIES = 184
PLANE = [(dx, dy) for dx in range(4) for dy in range(4) if dx or dy]


def dot(a, b):
    return jnp.dot(a, b, preferred_element_type=F32)


def dot_tn(a, b):
    return lax.dot_general(a, b, (((0,), (0,)), ((), ())), preferred_element_type=F32)


def dot_nt(a, b):
    return lax.dot_general(a, b, (((1,), (1,)), ((), ())), preferred_element_type=F32)


def split(value):
    high = value.astype(BF16)
    return high, (value - high.astype(F32)).astype(BF16)


def rows(start, count):
    return pl.ds(pl.multiple_of(start, count), count)


class Place:
    def __init__(self):
        me = lax.axis_index("seq")
        self.me = me
        self.x, self.y, self.z, self.c = me // 32, (me // 8) % 4, (me // 2) % 4, me % 2
        self.g = self.x * 4 + self.y
        self.sibling = me + 1 - 2 * self.c
        c = self.c
        self.l, self.l_step = self.z + c * (self.x - self.z), 2 + 30 * c
        self.p, self.p_step = self.x + c * (self.y - self.x), 32 - 24 * c
        self.q, self.q_step = self.y + c * (self.z - self.y), 8 - 6 * c
        self.l_sibling = self.x + c * (self.z - self.x)
        self.pq = self.p * 4 + self.q
        self.next = (me + 1) % DEVS
        self.prev = (me + DEVS - 1) % DEVS

    def line(self):
        for d in (1, 2, 3):
            zt = (self.z + d) % 4
            yield zt, self.me - 2 * self.z + 2 * zt

    def plane(self):
        for dx, dy in PLANE:
            xt, yt = (self.x + dx) % 4, (self.y + dy) % 4
            yield xt, yt, (xt * 4 + yt) * 8 + self.me % 8


    def sum_line(self):
        for d in (1, 2, 3):
            lt = (self.l + d) % 4
            yield lt, self.me + (lt - self.l) * self.l_step

    def sum_plane(self):
        for dp, dq in PLANE:
            pt, qt = (self.p + dp) % 4, (self.q + dq) % 4
            yield pt * 4 + qt, self.me + (pt - self.p) * self.p_step + (qt - self.q) * self.q_step


class Links:
    def __init__(self, send, recv):
        self.send, self.recv, self.sent = send, recv, []

    def start(self, src, dst, device, when=None):
        k = len(self.sent)
        copy = pltpu.make_async_remote_copy(
            src_ref=src,
            dst_ref=dst,
            send_sem=self.send.at[k],
            recv_sem=self.recv.at[k],
            device_id=(device,),
            device_id_type=MESH,
        )
        if when is None:
            copy.start()
        else:
            pl.when(when)(copy.start)
        self.sent.append((copy, when))
        return copy

    def finish(self):
        for copy, when in self.sent:
            if when is None:
                copy.wait_send()
            else:
                pl.when(when)(copy.wait_send)


def arrived(copies):
    for copy in copies:
        copy.wait_recv()


def greet(at):
    barrier = pltpu.get_barrier_semaphore()
    far = at.me + DEVS - 1 + 2 * at.c
    partners = [at.sibling, far % DEVS]
    partners += [dev for zt, dev in at.line()] + [dev for xt, yt, dev in at.plane()]
    for dy in (1, 2, 3):
        for zt, dev in at.line():
            partners.append(dev + (((at.y + dy) % 4) - at.y) * 8)
    for dev in partners:
        pl.semaphore_signal(barrier, inc=1, device_id=(dev,), device_id_type=MESH)
    return lambda: pl.semaphore_wait(barrier, len(partners))


def scan(at, links, state, out, sib, mine_c, zbuf, pbuf, ret, ebuf, give, reverse):
    mine, other = rows(at.c * 256, 256), rows((1 - at.c) * 256, 256)
    first = links.start(state.at[other], sib, at.sibling)
    yield
    arrived([first])
    chip = state[mine, :] + sib[...]
    for k in range(4):
        pack(mine_c.at[k], chip[k * 64 : (k + 1) * 64])
    copies = []
    for zt, dev in at.line():
        copies.append(links.start(mine_c.at[zt], zbuf.at[at.z], dev))
    zbuf[at.z] = mine_c[at.z]
    yield
    arrived(copies)
    parts = [unpack(zbuf.at[k]) for k in range(4)]
    pack(pbuf.at[at.g], parts[0] + parts[1] + parts[2] + parts[3])
    copies = []
    for dx, dy in PLANE:
        gt = ((at.x + dx) % 4) * 4 + (at.y + dy) % 4
        gs = ((at.x + 4 - dx) % 4) * 4 + (at.y + 4 - dy) % 4
        goes, comes = (gt < at.g, gs > at.g) if reverse else (gt > at.g, gs < at.g)
        copies.append((comes, links.start(pbuf.at[at.g], pbuf.at[at.g], gt * 8 + at.me % 8, goes)))
    yield
    for comes, copy in copies:
        pl.when(comes)(copy.wait_recv)
    total = jnp.zeros((64, HS), F32)
    for k in range(16):
        passed = (k > at.g) if reverse else (k < at.g)
        total = total + jnp.where(passed, unpack(pbuf.at[k]), 0.0)
    for k in range(3, -1, -1) if reverse else range(4):
        pack(ret.at[k], total)
        total = total + parts[k]
    copies = []
    for zt, dev in at.line():
        copies.append(links.start(ret.at[zt], ebuf.at[at.z], dev))
    ebuf[at.z] = ret[at.z]
    yield
    arrived(copies)
    first_core = at.c == (1 if reverse else 0)
    before = jnp.concatenate([unpack(ebuf.at[k]) for k in range(4)], axis=0)
    give[...] = before + jnp.where(first_core, state[mine, :], 0.0)
    last = links.start(give, out.at[mine], at.sibling)
    out[mine, :] = before + jnp.where(first_core, 0.0, sib[...])
    yield
    arrived([last])


def pack(ref, value):
    codes, exponents = code_of([value])
    ref[pl.ds(0, 64), :] = codes[0]
    ref[pl.ds(64, 16), :] = to_i16(jnp.broadcast_to(exponents[0], (16, 128)))


def unpack(ref):
    return number(ref[pl.ds(0, 64), :]) * powers(ref[pl.ds(64, 16), :])[:1]


def code_of(blocks):
    codes, exponents = [], []
    for value in blocks:
        most = jnp.max(jnp.abs(value), axis=0, keepdims=True)
        exponent = jnp.floor(jnp.log2(jnp.maximum(most, 1e-30))) + 1.0
        codes.append(jnp.round(value * jnp.exp2(14.0 - exponent)).astype(jnp.int32).astype(jnp.int16))
        exponents.append(exponent)
    return codes, exponents


def powers(tile):
    return jnp.exp2(tile.astype(jnp.int32).astype(F32) - 14.0)


def number(code):
    return code.astype(jnp.int32).astype(F32)


def to_i16(value):
    return value.astype(jnp.int32).astype(jnp.int16)


def reduce_all(at, links, src, r0, own, r1, zb, r2, pb, ag, pa, full):
    order = [(at.l + d) % 4 for d in (1, 2, 3, 0)]
    copies = []
    for d in (1, 2, 3, 0):
        k = (at.l_sibling + d) % 4
        copies.append(links.start(src.at[rows((1 - at.c) * 256 + k * 64, 64)], r0.at[k], at.sibling))
    yield
    line = []
    pad = jnp.zeros((8, 128), F32)
    for i, (lt, dev) in enumerate(at.sum_line()):
        arrived([copies[i]])
        blocks = [
            src[rows(at.c * 256 + lt * 64, 64), pl.ds(j * 128, 128)] + r0[lt, :, pl.ds(j * 128, 128)] for j in range(8)
        ]
        codes, exponents = code_of(blocks)
        for j in range(8):
            r1[i, pl.ds(j * 64, 64), :] = codes[j]
        r1[i, pl.ds(512, 16), :] = to_i16(jnp.concatenate(exponents + [pad], axis=0))
        line.append(links.start(r1.at[i], zb.at[i], dev))
    arrived([copies[3]])
    for j in range(8):
        own[pl.ds(j * 64, 64), :] = (
            src[rows(at.c * 256 + at.l * 64, 64), pl.ds(j * 128, 128)] + r0[at.l, :, pl.ds(j * 128, 128)]
        )
    yield
    arrived(line)
    scales = [powers(zb[i, pl.ds(512, 16), :]) for i in range(3)]
    pad = jnp.zeros((14, 128), F32)
    for k in range(16):
        pk, qk = k // 4, k % 4
        blocks = []
        for j in (2 * qk, 2 * qk + 1):
            part = pl.ds(j * 64 + pk * 16, 16)
            value = own[part, :]
            for i in range(3):
                value = value + number(zb[i, part, :]) * scales[i][j : j + 1]
            blocks.append(value)
        codes, exponents = code_of(blocks)
        r2[k, pl.ds(0, 16), :] = codes[0]
        r2[k, pl.ds(16, 16), :] = codes[1]
        r2[k, pl.ds(32, 16), :] = to_i16(jnp.concatenate(exponents + [pad], axis=0))
    plane = []
    for i, (k, dev) in enumerate(at.sum_plane()):
        plane.append(links.start(r2.at[k], pb.at[i], dev))
    yield
    arrived(plane)
    scale = powers(r2[at.pq, pl.ds(32, 16), :])
    total = [number(r2[at.pq, pl.ds(16 * b, 16), :]) * scale[b : b + 1] for b in range(2)]
    for i in range(15):
        scale = powers(pb[i, pl.ds(32, 16), :])
        total = [total[b] + number(pb[i, pl.ds(16 * b, 16), :]) * scale[b : b + 1] for b in range(2)]
    codes, exponents = code_of(total)
    row = lax.broadcasted_iota(jnp.int32, (16, 128), 0) - 2 * (at.pq % 8)
    ag[pl.ds(0, 16), :] = codes[0]
    ag[pl.ds(16, 16), :] = codes[1]
    ag[pl.ds(32, 16), :] = to_i16(jnp.where(row == 0, exponents[0], jnp.where(row == 1, exponents[1], 0.0)))
    plane = []
    for k, dev in at.sum_plane():
        plane.append(links.start(ag, pa.at[at.pq], dev))
    pa[at.pq] = ag[...]
    yield
    arrived(plane)
    mine = full.at[at.c, at.l]
    for k in range(16):
        mine[pl.ds(k * 32, 32), :] = pa[k, pl.ds(0, 32), :]
    for b in range(2):
        tile = pa[8 * b, pl.ds(32, 16), :].astype(jnp.int32)
        for k in range(1, 8):
            tile = tile + pa[8 * b + k, pl.ds(32, 16), :].astype(jnp.int32)
        mine[pl.ds(512 + 16 * b, 16), :] = tile.astype(jnp.int16)
    line = []
    for lt, dev in at.sum_line():
        line.append(links.start(mine, mine, dev))
    other = [links.start(mine, mine, at.sibling)]
    yield
    for d in (1, 2, 3):
        arrived([line[d - 1]])
        k = (at.l + 4 - d) % 4
        other.append(links.start(full.at[at.c, k], full.at[at.c, k], at.sibling))
    yield
    arrived(other)


def decode(early_in, late_in, small, qkv_out, out_out, head_out, gain_out, sib_out, early, late, qkv, out, load, store):
    loads, stores = [], []
    for k in range(8):
        for i, (src, dst) in enumerate(((early_in, early), (late_in, late))):
            loads.append(pltpu.make_async_copy(src.at[k // 4, k % 4], dst.at[k], load.at[2 * k + i]))
            loads[-1].start()
    for k in range(8):
        for i, (full, first) in enumerate(((early, 0), (late, 1024))):
            loads[2 * k + i].wait()
            scales = [powers(full[k, pl.ds(512 + 16 * b, 16), :]) for b in range(2)]
            for g in range(16):
                for b in range(2):
                    e = 2 * (g % 8) + b
                    value = number(full[k, pl.ds(g * 32 + b * 16, 16), :]) * scales[g // 8][e : e + 1]
                    column = first + (g % 4) * 256 + b * 128
                    to, column = (out, column) if column < D else (qkv, column - D)
                    to[pl.ds(k * 64 + g // 4 * 16, 16), pl.ds(column, 128)] = value
        part = pl.ds(k * 64, 64)
        for i, (src, dst) in enumerate(((qkv, qkv_out), (out, out_out))):
            stores.append(pltpu.make_async_copy(src.at[part], dst.at[part], store.at[2 * k + i]))
            stores[-1].start()
    head_out[...] = small[pl.ds(0, 8), :]
    gain_out[...] = small[pl.ds(8, 1), :]
    sib_out[...] = small[pl.ds(16, 8), :]
    for copy in stores:
        copy.wait()


def reduce_small(at, links, xs, xo, x0, x1, xz, xp):
    mine, other = rows(at.c * 16, 16), rows((1 - at.c) * 16, 16)
    first = links.start(xs.at[other], x0, at.sibling)
    yield
    arrived([first])
    total = xs[mine, :] + x0[...]
    for k in range(4):
        x1[k] = total[:, k * 128 : (k + 1) * 128]
    copies = []
    for lt, dev in at.sum_line():
        copies.append(links.start(x1.at[lt], xz.at[at.l], dev))
    xz[at.l] = x1[at.l]
    yield
    arrived(copies)
    xp[at.pq] = xz[0] + xz[1] + xz[2] + xz[3]
    copies = []
    for k, dev in at.sum_plane():
        copies.append(links.start(xp.at[at.pq], xp.at[at.pq], dev))
    yield
    arrived(copies)
    total = xp[0]
    for k in range(1, 16):
        total = total + xp[k]
    place = xo.at[mine, rows(at.l * 128, 128)]
    place[...] = total
    copies = []
    for lt, dev in at.sum_line():
        copies.append(links.start(place, place, dev))
    yield
    arrived(copies)
    last = links.start(xo.at[mine], xo.at[mine], at.sibling)
    yield
    arrived([last])


def step(generator):
    for _ in generator:
        return True
    return False


def finish(generator):
    while step(generator):
        pass


def head(h, part=0):
    return pl.ds(part * D + h * HS, HS)


def block(b):
    return pl.ds(b * RB, RB)


def lower(b):
    row = lax.broadcasted_iota(jnp.int32, (RB, (b + 1) * RB), 0) + b * RB
    col = lax.broadcasted_iota(jnp.int32, (RB, (b + 1) * RB), 1)
    return col <= row


def kernel(
    parents, counts_in, occupancy_in, sib_in, gain_in, w_qkv_in, w_out_in, w_head_in,
    e_full, l_full, small_out,
    window, ends, offz, offp, offs, inputs, inv_in, normed, packed, onehot,
    scores, numer, resid, inv_out, final, attended, d_logits, d_resid, d_resid_b, wide, grads, d_packed,
    d_local, states, prefix, qstates, suffix,
    f_sib, f_chip, f_z, f_p, f_ret, f_e, f_give,
    b_sib, b_chip, b_z, b_p, b_ret, b_e, b_give,
    early, e_r0, e_own, e_r1, e_z, e_r2, e_p, e_ag, e_pa,
    late, l_r0, l_own, l_r1, l_z, l_r2, l_p, l_ag, l_pa,
    small, x0, x1, xz, xp,
    counts, occupancy, sib_table, gain, w_qkv, w_out, w_head, pair_rows, pair_kv, moved,
    send, recv, load,
):
    at = Place()
    links = Links(send, recv)
    own = pl.ds(PAR, PAR)
    pairs = [
        (counts_in, counts), (parents, window.at[own]), (sib_in, sib_table), (gain_in, gain), (w_qkv_in, w_qkv),
        (occupancy_in, occupancy), (w_out_in, w_out), (w_head_in, w_head),
    ]
    loads = [pltpu.make_async_copy(src, dst, load.at[i]) for i, (src, dst) in enumerate(pairs)]
    for copy in loads:
        copy.start()
    all_here = greet(at)

    loads[0].wait()
    count = jnp.broadcast_to(counts[...].astype(F32), (16, PAR))
    whole = jnp.sum(count[:8], axis=1, keepdims=True)
    offs[0] = jnp.broadcast_to(whole, (8, 128))
    tri = (
        lax.broadcasted_iota(jnp.int32, (PAR, PAR), 0) <= lax.broadcasted_iota(jnp.int32, (PAR, PAR), 1)
    ).astype(BF16)
    local_ends = dot(count.astype(BF16), tri)[:8]
    ends[1, :8] = local_ends
    ends[1, 8:] = count[:8]
    count_col = count[:8].T[:, :1]
    start_col = (local_ends - count[:8]).T[:, :1]
    for copy in loads[1:]:
        copy.wait()
    for r in range(8):
        value = (window[own, :].astype(F32) + sib_table[r : r + 1, :].astype(F32)).astype(BF16).astype(F32)
        inverse = lax.rsqrt(jnp.mean(value * value, axis=-1, keepdims=True) + 1e-06)
        inverse = jnp.where(count_col > float(r), inverse, 0.0)
        pair_rows[pl.ds(r * PAR, PAR), :] = (value * inverse * gain[...]).astype(BF16)
    pair_kv[...] = dot(pair_rows[...], w_qkv[:, pl.ds(D, 2 * D)]).astype(BF16)
    for h in range(HEADS):
        states[pl.ds(h * HS, HS), :] = dot_tn(pair_kv[:, head(h)], pair_kv[:, head(h, 1)])
    all_here()

    first = links.start(offs.at[0], offs.at[1], at.sibling)
    forward = scan(at, links, states, prefix, f_sib, f_chip, f_z, f_p, f_ret, f_e, f_give, False)
    step(forward)
    arrived([first])
    offset = jnp.where(at.c == 1, offs[1], 0.0)
    offz[at.z] = offs[0] + offs[1]
    copies = [links.start(offz.at[at.z], offz.at[at.z], dev) for zt, dev in at.line()]
    step(forward)
    halo = [
        links.start(ends.at[1], ends.at[0], at.next),
        links.start(ends.at[1], ends.at[2], at.prev),
        links.start(parents, window.at[pl.ds(0, PAR)], at.next),
        links.start(parents, window.at[pl.ds(2 * PAR, PAR)], at.prev),
    ]
    arrived(copies)
    offp[at.g] = offz[0] + offz[1] + offz[2] + offz[3]
    copies = [links.start(offp.at[at.g], offp.at[at.g], dev) for xt, yt, dev in at.plane()]
    for k in range(4):
        offset = offset + jnp.where(k < at.z, offz[k], 0.0)
    step(forward)
    arrived(copies)
    for k in range(16):
        offset = offset + jnp.where(k < at.g, offp[k], 0.0)
    shift = (at.me * N).astype(F32) - offset[:1, :1]
    arrived(halo)

    own_total = whole[:1, :1]
    low_total = ends[0, :1, PAR - 1 :]
    end_row = jnp.concatenate([ends[0, :1] - low_total, local_ends[:1], ends[2, :1] + own_total], axis=1)
    count_row = jnp.concatenate([ends[0, 8:9], count[:1], ends[2, 8:9]], axis=1)
    start_row = end_row - count_row
    lanes8 = lax.broadcasted_iota(jnp.int32, (128, 8), 0)
    spread = (lanes8 == lax.broadcasted_iota(jnp.int32, (128, 8), 1) + 16).astype(BF16)
    sib_rows = dot(spread, sib_table[...]).astype(BF16)
    lane = lax.broadcasted_iota(jnp.int32, (RB, 128), 1)
    for b in range(BLOCKS):
        place = lax.broadcasted_iota(jnp.int32, (RB, 1), 0).astype(F32) + (shift + float(b * RB))
        child = (start_row <= place) & (place < end_row)
        chosen = jnp.where(child, 1.0, 0.0).astype(BF16)
        start_of = jnp.sum(jnp.where(child, start_row, 0.0), axis=1, keepdims=True)
        rank = (place - start_of).astype(jnp.int32)
        hot = (rank + 16 == lane).astype(F32).astype(BF16)
        onehot[block(b), :] = hot
        value = (dot(chosen, window[...]) + dot(hot, sib_rows)).astype(BF16)
        inputs[block(b), :] = value
        value = value.astype(F32)
        inverse = lax.rsqrt(jnp.mean(value * value, axis=-1, keepdims=True) + 1e-06)
        inv_in[block(b), :] = inverse
        normed[block(b), :] = (value * inverse * gain[...]).astype(BF16)
    packed[...] = dot(normed[...], w_qkv[...]).astype(BF16)
    step(forward)

    for h in range(HEADS):
        for b in range(BLOCKS):
            keys, values = packed[: (b + 1) * RB, head(h, 1)], packed[: (b + 1) * RB, head(h, 2)]
            score = jnp.where(lower(b), dot_nt(packed[block(b), head(h)], keys), 0.0).astype(BF16)
            scores[h, block(b), : (b + 1) * RB] = score
            numer[block(b), head(h)] = dot(score, values)
        if h == 2:
            step(forward)
    for r in range(8):
        part = pl.ds(r * PAR, PAR)
        before = jnp.where(start_col + float(r) < shift, 1.0, 0.0)
        pair_rows[part, :] = (pair_kv[part, pl.ds(0, D)].astype(F32) * before).astype(BF16)
    place = lax.broadcasted_iota(jnp.int32, (N, 1), 0).astype(F32) + shift
    wide[...] = packed[:, pl.ds(D, D)].astype(F32) * jnp.where(place < 0.0, -1.0, 0.0)
    for h in range(HEADS):
        moved[pl.ds(h * HS, HS), :] = dot_tn(pair_rows[:, head(h)], pair_kv[:, head(h, 1)]) + dot_tn(
            wide[:, head(h)].astype(BF16), packed[:, head(h, 2)]
        )
    finish(forward)
    prefix[...] += moved[...]

    for h in range(HEADS):
        high, low = split(prefix[pl.ds(h * HS, HS), :])
        q = packed[:, head(h)]
        wide[:, head(h)] = dot(q, high) + dot(q, low)
    scale = float(DEVS * N) ** (-0.5)
    lane8 = lax.broadcasted_iota(jnp.int32, (RB, 8), 1)
    symbols = jnp.broadcast_to(occupancy[...].astype(F32), (8, N)).T.astype(jnp.int32)
    inv_heads = []
    for b in range(BLOCKS):
        for h in range(HEADS):
            value = numer[block(b), head(h)] + wide[block(b), head(h)]
            numer[block(b), head(h)] = value
            inverse = lax.rsqrt(jnp.mean(value * value, axis=-1, keepdims=True) + 1e-05)
            attended[block(b), head(h)] = (value * inverse).astype(BF16)
            inv_heads.append(inverse)
    wide[...] = dot(attended[...], w_out[...])
    for b in range(BLOCKS):
        value = inputs[block(b), :].astype(F32) + wide[block(b), :]
        resid[block(b), :] = value
        inverse = lax.rsqrt(jnp.mean(value * value, axis=-1, keepdims=True) + 1e-06)
        inv_out[block(b), :] = inverse
        last = (value * inverse).astype(BF16)
        final[block(b), :] = last
        logits = dot_nt(last, w_head[...])
        target = ((symbols[b * RB : (b + 1) * RB] >> lane8) & 1).astype(F32)
        small_grad = ((jax.nn.sigmoid(logits) - target) * scale).astype(BF16)
        d_logits[block(b), :] = small_grad
        d_final = dot(small_grad, w_head[...])
        mean = jnp.mean(d_final * value, axis=-1, keepdims=True)
        d_value = inverse * d_final - value * (inverse * inverse * inverse) * mean
        d_resid[block(b), :] = d_value
        d_resid_b[block(b), :] = d_value.astype(BF16)
    wide[...] = dot_nt(d_resid_b[...], w_out[...])
    for b in range(BLOCKS):
        for h in range(HEADS):
            piece, value, inverse = wide[block(b), head(h)], numer[block(b), head(h)], inv_heads[b * HEADS + h]
            mean = jnp.mean(piece * value, axis=-1, keepdims=True)
            grads[block(b), head(h)] = (inverse * piece - value * (inverse * inverse * inverse) * mean).astype(BF16)
    for h in range(HEADS):
        qstates[pl.ds(h * HS, HS), :] = dot_tn(packed[:, head(h)], grads[:, head(h)])

    backward = scan(at, links, qstates, suffix, b_sib, b_chip, b_z, b_p, b_ret, b_e, b_give, True)
    step(backward)
    early[:, pl.ds(0, D)] = dot_tn(attended[...], d_resid_b[...])
    step(backward)
    for h in range(HEADS):
        high, low = split(prefix[pl.ds(h * HS, HS), :])
        g = grads[:, head(h)]
        wide[:, head(h)] = dot_nt(g, high) + dot_nt(g, low)
    d_local[...] = jnp.zeros_like(d_local)
    for h in range(HEADS):
        for b in range(BLOCKS):
            upto = pl.ds(0, (b + 1) * RB)
            g, q = grads[block(b), head(h)], packed[block(b), head(h)]
            back = jnp.where(lower(b), dot_nt(g, packed[upto, head(h, 2)]), 0.0).astype(BF16)
            dq = dot(back, packed[upto, head(h, 1)]) + wide[block(b), head(h)]
            d_packed[block(b), head(h)] = dq.astype(BF16)
            d_local[upto, head(h)] += dot_tn(back, q)
            d_local[upto, head(h, 1)] += dot_tn(scores[h, block(b), upto], g)
        if h == 1:
            step(backward)
    step(backward)
    early[:, pl.ds(D, D)] = dot_tn(normed[...], d_packed[:, pl.ds(0, D)])
    early_sum = reduce_all(at, links, early, e_r0, e_own, e_r1, e_z, e_r2, e_p, e_ag, e_pa, e_full)
    step(early_sum)
    wide[...] = dot_nt(d_packed[:, pl.ds(0, D)], w_qkv[:, pl.ds(0, D)])
    step(backward)
    step(early_sum)
    finish(backward)

    for h in range(HEADS):
        high, low = split(suffix[pl.ds(h * HS, HS), :])
        k, v = packed[:, head(h, 1)], packed[:, head(h, 2)]
        d_packed[:, head(h, 1)] = (d_local[:, head(h)] + dot_nt(v, high) + dot_nt(v, low)).astype(BF16)
        d_packed[:, head(h, 2)] = (d_local[:, head(h, 1)] + dot(k, high) + dot(k, low)).astype(BF16)
    late[...] = dot_tn(normed[...], d_packed[:, pl.ds(D, 2 * D)])
    late_sum = reduce_all(at, links, late, l_r0, l_own, l_r1, l_z, l_r2, l_p, l_ag, l_pa, l_full)
    step(late_sum)
    step(late_sum)
    step(early_sum)
    wide[...] += dot_nt(d_packed[:, pl.ds(D, 2 * D)], w_qkv[:, pl.ds(D, 2 * D)])
    grad_gain = jnp.zeros((1, D), F32)
    grad_sib = jnp.zeros((128, D), F32)
    for b in range(BLOCKS):
        value, inverse, slope = inputs[block(b), :].astype(F32), inv_in[block(b), :], wide[block(b), :]
        grad_gain = grad_gain + jnp.sum(slope * value * inverse, axis=0, keepdims=True)
        scaled = slope * gain[...]
        mean = jnp.mean(scaled * value, axis=-1, keepdims=True)
        d_in = inverse * scaled - value * (inverse * inverse * inverse) * mean + d_resid[block(b), :]
        high, low = split(d_in)
        grad_sib = grad_sib + dot_tn(onehot[block(b), :], high) + dot_tn(onehot[block(b), :], low)
    small[pl.ds(0, 8), :] = dot_tn(d_logits[...], final[...])
    small[pl.ds(8, 8), :] = jnp.broadcast_to(grad_gain, (8, D))
    small[pl.ds(16, 16), :] = grad_sib[16:32]
    small_sum = reduce_small(at, links, small, small_out, x0, x1, xz, xp)
    step(small_sum)
    more = True
    while more:
        more = step(late_sum)
        step(small_sum)
        step(early_sum)
    finish(early_sum)
    finish(small_sum)
    links.finish()


def vm(shape, dtype=F32):
    return pltpu.VMEM(shape, dtype)


def scan_buffers():
    coded = [vm((k, 80, 128), jnp.int16) for k in (4, 4, 16, 4, 4)]
    return [vm((256, HS)), *coded, vm((256, HS))]


def sum_buffers():
    i16 = jnp.int16
    return [
        vm((N, 1024)), vm((4, 64, 1024)), vm((512, 128)), vm((3, 528, 128), i16), vm((3, 528, 128), i16),
        vm((16, 48, 128), i16), vm((15, 48, 128), i16), vm((48, 128), i16), vm((16, 48, 128), i16),
    ]


def shards(parent_rows, counts, occupancy, sib_table, gain, w_qkv, w_out, w_head):
    scratch = [
        vm((3 * PAR, D), BF16), vm((3, 16, PAR)), vm((4, 8, 128)), vm((16, 8, 128)), vm((2, 8, 128)),
        vm((N, D), BF16), vm((N, 1)), vm((N, D), BF16), vm((N, 3 * D), BF16), vm((N, 128), BF16),
        vm((HEADS, N, N), BF16), vm((N, D)), vm((N, D)), vm((N, 1)), vm((N, D), BF16), vm((N, D), BF16),
        vm((N, 8), BF16), vm((N, D)), vm((N, D), BF16), vm((N, D)), vm((N, D), BF16), vm((N, 3 * D), BF16),
        vm((N, 2 * D)), vm((N, HS)), vm((N, HS)), vm((N, HS)), vm((N, HS)),
        *scan_buffers(), *scan_buffers(), *sum_buffers(), *sum_buffers(),
        vm((32, D)), vm((16, D)), vm((4, 16, 128)), vm((4, 16, 128)), vm((16, 16, 128)),
        vm((1, PAR), jnp.int32), vm((1, N), jnp.int32), vm((8, D), BF16), vm((1, D)), vm((D, 3 * D), BF16), vm((D, D), BF16),
        vm((8, D), BF16), vm((8 * PAR, D), BF16), vm((8 * PAR, 2 * D), BF16), vm((N, HS)),
        pltpu.SemaphoreType.DMA((COPIES,)), pltpu.SemaphoreType.DMA((COPIES,)), pltpu.SemaphoreType.DMA((8,)),
    ]
    spec = pl.BlockSpec(memory_space=pltpu.VMEM)
    codes = jax.ShapeDtypeStruct((2, 4, 544, 128), jnp.int16)
    early, late, small = pl.pallas_call(
        kernel,
        out_shape=[codes, codes, jax.ShapeDtypeStruct((32, D), F32)],
        in_specs=[pl.BlockSpec(memory_space=pltpu.HBM)] * 8,
        out_specs=[spec] * 3,
        scratch_shapes=scratch,
        compiler_params=pltpu.CompilerParams(
            collective_id=0, has_side_effects=True, vmem_limit_bytes=58 * 1024 * 1024
        ),
        name="train_step",
    )(
        parent_rows, counts.reshape(1, PAR), occupancy.reshape(1, N), sib_table, gain.reshape(1, D),
        w_qkv, w_out, w_head.T,
    )
    hbm = pl.BlockSpec(memory_space=pl.ANY)
    shapes = [(D, 3 * D), (D, D), (8, D), (1, D), (8, D)]
    grad_qkv, grad_out, grad_head, grad_gain, grad_sib = pl.pallas_call(
        decode,
        in_specs=[hbm, hbm, spec],
        out_specs=[hbm, hbm, spec, spec, spec],
        out_shape=[jax.ShapeDtypeStruct(shape, F32) for shape in shapes],
        scratch_shapes=[
            vm((8, 544, 128), jnp.int16), vm((8, 544, 128), jnp.int16), vm((D, 3 * D)), vm((D, D)),
            pltpu.SemaphoreType.DMA((16,)), pltpu.SemaphoreType.DMA((16,)),
        ],
        compiler_params=pltpu.CompilerParams(vmem_limit_bytes=58 * 1024 * 1024),
        name="decode",
    )(early, late, small)
    return grad_qkv, grad_out, grad_head.T, grad_gain.reshape(D), grad_sib


def solution(mesh):
    placed = (P("seq", None), P("seq"), P("seq"), P(), P(), P(), P(), P())
    return jax.shard_map(
        shards, mesh=mesh, in_specs=placed, out_specs=(P(), P(), P(), P(), P()), check_vma=False
    )
```

```python
import jax
import jax.numpy as jnp
from jax import lax
from jax.experimental import pallas as pl
from jax.experimental.pallas import tpu as pltpu
from jax.sharding import PartitionSpec as P

MESH = pl.DeviceIdType.MESH
F32, BF16 = jnp.float32, jnp.bfloat16
HEADS, HS, D = 4, 128, 512
N, PAR, DEVS = 512, 256, 128
RB = 128
BLOCKS = N // RB
COPIES = 184
PLANE = [(dx, dy) for dx in range(4) for dy in range(4) if dx or dy]


def dot(a, b):
    return jnp.dot(a, b, preferred_element_type=F32)


def dot_tn(a, b):
    return lax.dot_general(a, b, (((0,), (0,)), ((), ())), preferred_element_type=F32)


def dot_nt(a, b):
    return lax.dot_general(a, b, (((1,), (1,)), ((), ())), preferred_element_type=F32)


def split(value):
    high = value.astype(BF16)
    return high, (value - high.astype(F32)).astype(BF16)


def rows(start, count):
    return pl.ds(pl.multiple_of(start, count), count)


class Place:
    def __init__(self):
        me = lax.axis_index("seq")
        self.me = me
        self.x, self.y, self.z, self.c = me // 32, (me // 8) % 4, (me // 2) % 4, me % 2
        self.g = self.x * 4 + self.y
        self.sibling = me + 1 - 2 * self.c
        c = self.c
        self.l, self.l_step = self.z + c * (self.x - self.z), 2 + 30 * c
        self.p, self.p_step = self.x + c * (self.y - self.x), 32 - 24 * c
        self.q, self.q_step = self.y + c * (self.z - self.y), 8 - 6 * c
        self.l_sibling = self.x + c * (self.z - self.x)
        self.pq = self.p * 4 + self.q
        self.next = (me + 1) % DEVS
        self.prev = (me + DEVS - 1) % DEVS

    def line(self):
        for d in (1, 2, 3):
            zt = (self.z + d) % 4
            yield zt, self.me - 2 * self.z + 2 * zt

    def plane(self):
        for dx, dy in PLANE:
            xt, yt = (self.x + dx) % 4, (self.y + dy) % 4
            yield xt, yt, (xt * 4 + yt) * 8 + self.me % 8


    def sum_line(self):
        for d in (1, 2, 3):
            lt = (self.l + d) % 4
            yield lt, self.me + (lt - self.l) * self.l_step

    def sum_plane(self):
        for dp, dq in PLANE:
            pt, qt = (self.p + dp) % 4, (self.q + dq) % 4
            yield pt * 4 + qt, self.me + (pt - self.p) * self.p_step + (qt - self.q) * self.q_step


class Links:
    def __init__(self, send, recv):
        self.send, self.recv, self.sent = send, recv, []

    def start(self, src, dst, device, when=None):
        k = len(self.sent)
        copy = pltpu.make_async_remote_copy(
            src_ref=src,
            dst_ref=dst,
            send_sem=self.send.at[k],
            recv_sem=self.recv.at[k],
            device_id=(device,),
            device_id_type=MESH,
        )
        if when is None:
            copy.start()
        else:
            pl.when(when)(copy.start)
        self.sent.append((copy, when))
        return copy

    def finish(self):
        for copy, when in self.sent:
            if when is None:
                copy.wait_send()
            else:
                pl.when(when)(copy.wait_send)


def arrived(copies):
    for copy in copies:
        copy.wait_recv()


def greet(at):
    barrier = pltpu.get_barrier_semaphore()
    far = at.me + DEVS - 1 + 2 * at.c
    partners = [at.sibling, far % DEVS]
    partners += [dev for zt, dev in at.line()] + [dev for xt, yt, dev in at.plane()]
    for dy in (1, 2, 3):
        for zt, dev in at.line():
            partners.append(dev + (((at.y + dy) % 4) - at.y) * 8)
    for dev in partners:
        pl.semaphore_signal(barrier, inc=1, device_id=(dev,), device_id_type=MESH)
    return lambda: pl.semaphore_wait(barrier, len(partners))


def scan(at, links, state, out, sib, mine_c, zbuf, pbuf, ret, ebuf, give, reverse):
    mine, other = rows(at.c * 256, 256), rows((1 - at.c) * 256, 256)
    first = links.start(state.at[other], sib, at.sibling)
    yield
    arrived([first])
    chip = state[mine, :] + sib[...]
    for k in range(4):
        pack(mine_c.at[k], chip[k * 64 : (k + 1) * 64])
    copies = []
    for zt, dev in at.line():
        copies.append(links.start(mine_c.at[zt], zbuf.at[at.z], dev))
    zbuf[at.z] = mine_c[at.z]
    yield
    arrived(copies)
    parts = [unpack(zbuf.at[k]) for k in range(4)]
    pack(pbuf.at[at.g], parts[0] + parts[1] + parts[2] + parts[3])
    copies = []
    for dx, dy in PLANE:
        gt = ((at.x + dx) % 4) * 4 + (at.y + dy) % 4
        gs = ((at.x + 4 - dx) % 4) * 4 + (at.y + 4 - dy) % 4
        goes, comes = (gt < at.g, gs > at.g) if reverse else (gt > at.g, gs < at.g)
        copies.append((comes, links.start(pbuf.at[at.g], pbuf.at[at.g], gt * 8 + at.me % 8, goes)))
    yield
    for comes, copy in copies:
        pl.when(comes)(copy.wait_recv)
    total = jnp.zeros((64, HS), F32)
    for k in range(16):
        passed = (k > at.g) if reverse else (k < at.g)
        total = total + jnp.where(passed, unpack(pbuf.at[k]), 0.0)
    for k in range(3, -1, -1) if reverse else range(4):
        pack(ret.at[k], total)
        total = total + parts[k]
    copies = []
    for zt, dev in at.line():
        copies.append(links.start(ret.at[zt], ebuf.at[at.z], dev))
    ebuf[at.z] = ret[at.z]
    yield
    arrived(copies)
    first_core = at.c == (1 if reverse else 0)
    before = jnp.concatenate([unpack(ebuf.at[k]) for k in range(4)], axis=0)
    give[...] = before + jnp.where(first_core, state[mine, :], 0.0)
    last = links.start(give, out.at[mine], at.sibling)
    out[mine, :] = before + jnp.where(first_core, 0.0, sib[...])
    yield
    arrived([last])


def pack(ref, value):
    codes, exponents = code_of([value])
    ref[pl.ds(0, 64), :] = codes[0]
    ref[pl.ds(64, 16), :] = to_i16(jnp.broadcast_to(exponents[0], (16, 128)))


def unpack(ref):
    return number(ref[pl.ds(0, 64), :]) * powers(ref[pl.ds(64, 16), :])[:1]


def code_of(blocks):
    codes, exponents = [], []
    for value in blocks:
        most = jnp.max(jnp.abs(value), axis=0, keepdims=True)
        exponent = jnp.floor(jnp.log2(jnp.maximum(most, 1e-30))) + 1.0
        codes.append(jnp.round(value * jnp.exp2(14.0 - exponent)).astype(jnp.int32).astype(jnp.int16))
        exponents.append(exponent)
    return codes, exponents


def powers(tile):
    return jnp.exp2(tile.astype(jnp.int32).astype(F32) - 14.0)


def number(code):
    return code.astype(jnp.int32).astype(F32)


def to_i16(value):
    return value.astype(jnp.int32).astype(jnp.int16)


def reduce_all(at, links, src, r0, own, r1, zb, r2, pb, ag, pa, full):
    order = [(at.l + d) % 4 for d in (1, 2, 3, 0)]
    copies = []
    for d in (1, 2, 3, 0):
        k = (at.l_sibling + d) % 4
        copies.append(links.start(src.at[rows((1 - at.c) * 256 + k * 64, 64)], r0.at[k], at.sibling))
    yield
    line = []
    pad = jnp.zeros((8, 128), F32)
    for i, (lt, dev) in enumerate(at.sum_line()):
        arrived([copies[i]])
        blocks = [
            src[rows(at.c * 256 + lt * 64, 64), pl.ds(j * 128, 128)] + r0[lt, :, pl.ds(j * 128, 128)] for j in range(8)
        ]
        codes, exponents = code_of(blocks)
        for j in range(8):
            r1[i, pl.ds(j * 64, 64), :] = codes[j]
        r1[i, pl.ds(512, 16), :] = to_i16(jnp.concatenate(exponents + [pad], axis=0))
        line.append(links.start(r1.at[i], zb.at[i], dev))
    arrived([copies[3]])
    for j in range(8):
        own[pl.ds(j * 64, 64), :] = (
            src[rows(at.c * 256 + at.l * 64, 64), pl.ds(j * 128, 128)] + r0[at.l, :, pl.ds(j * 128, 128)]
        )
    yield
    arrived(line)
    scales = [powers(zb[i, pl.ds(512, 16), :]) for i in range(3)]
    pad = jnp.zeros((14, 128), F32)
    for k in range(16):
        pk, qk = k // 4, k % 4
        blocks = []
        for j in (2 * qk, 2 * qk + 1):
            part = pl.ds(j * 64 + pk * 16, 16)
            value = own[part, :]
            for i in range(3):
                value = value + number(zb[i, part, :]) * scales[i][j : j + 1]
            blocks.append(value)
        codes, exponents = code_of(blocks)
        r2[k, pl.ds(0, 16), :] = codes[0]
        r2[k, pl.ds(16, 16), :] = codes[1]
        r2[k, pl.ds(32, 16), :] = to_i16(jnp.concatenate(exponents + [pad], axis=0))
    plane = []
    for i, (k, dev) in enumerate(at.sum_plane()):
        plane.append(links.start(r2.at[k], pb.at[i], dev))
    yield
    arrived(plane)
    scale = powers(r2[at.pq, pl.ds(32, 16), :])
    total = [number(r2[at.pq, pl.ds(16 * b, 16), :]) * scale[b : b + 1] for b in range(2)]
    for i in range(15):
        scale = powers(pb[i, pl.ds(32, 16), :])
        total = [total[b] + number(pb[i, pl.ds(16 * b, 16), :]) * scale[b : b + 1] for b in range(2)]
    codes, exponents = code_of(total)
    row = lax.broadcasted_iota(jnp.int32, (16, 128), 0) - 2 * (at.pq % 8)
    ag[pl.ds(0, 16), :] = codes[0]
    ag[pl.ds(16, 16), :] = codes[1]
    ag[pl.ds(32, 16), :] = to_i16(jnp.where(row == 0, exponents[0], jnp.where(row == 1, exponents[1], 0.0)))
    plane = []
    for k, dev in at.sum_plane():
        plane.append(links.start(ag, pa.at[at.pq], dev))
    pa[at.pq] = ag[...]
    yield
    arrived(plane)
    mine = full.at[at.c, at.l]
    for k in range(16):
        mine[pl.ds(k * 32, 32), :] = pa[k, pl.ds(0, 32), :]
    for b in range(2):
        tile = pa[8 * b, pl.ds(32, 16), :].astype(jnp.int32)
        for k in range(1, 8):
            tile = tile + pa[8 * b + k, pl.ds(32, 16), :].astype(jnp.int32)
        mine[pl.ds(512 + 16 * b, 16), :] = tile.astype(jnp.int16)
    line = []
    for lt, dev in at.sum_line():
        line.append(links.start(mine, mine, dev))
    other = [links.start(mine, mine, at.sibling)]
    yield
    for d in (1, 2, 3):
        arrived([line[d - 1]])
        k = (at.l + 4 - d) % 4
        other.append(links.start(full.at[at.c, k], full.at[at.c, k], at.sibling))
    yield
    arrived(other)


def decode(early_in, late_in, small, qkv_out, out_out, head_out, gain_out, sib_out, early, late, qkv, out, load, store):
    loads, stores = [], []
    for k in range(8):
        for i, (src, dst) in enumerate(((early_in, early), (late_in, late))):
            loads.append(pltpu.make_async_copy(src.at[k // 4, k % 4], dst.at[k], load.at[2 * k + i]))
            loads[-1].start()
    for k in range(8):
        for i, (full, first) in enumerate(((early, 0), (late, 1024))):
            loads[2 * k + i].wait()
            scales = [powers(full[k, pl.ds(512 + 16 * b, 16), :]) for b in range(2)]
            for g in range(16):
                for b in range(2):
                    e = 2 * (g % 8) + b
                    value = number(full[k, pl.ds(g * 32 + b * 16, 16), :]) * scales[g // 8][e : e + 1]
                    column = first + (g % 4) * 256 + b * 128
                    to, column = (out, column) if column < D else (qkv, column - D)
                    to[pl.ds(k * 64 + g // 4 * 16, 16), pl.ds(column, 128)] = value
        part = pl.ds(k * 64, 64)
        for i, (src, dst) in enumerate(((qkv, qkv_out), (out, out_out))):
            stores.append(pltpu.make_async_copy(src.at[part], dst.at[part], store.at[2 * k + i]))
            stores[-1].start()
    head_out[...] = small[pl.ds(0, 8), :]
    gain_out[...] = small[pl.ds(8, 1), :]
    sib_out[...] = small[pl.ds(16, 8), :]
    for copy in stores:
        copy.wait()


def reduce_small(at, links, xs, xo, x0, x1, xz, xp):
    mine, other = rows(at.c * 16, 16), rows((1 - at.c) * 16, 16)
    first = links.start(xs.at[other], x0, at.sibling)
    yield
    arrived([first])
    total = xs[mine, :] + x0[...]
    for k in range(4):
        x1[k] = total[:, k * 128 : (k + 1) * 128]
    copies = []
    for lt, dev in at.sum_line():
        copies.append(links.start(x1.at[lt], xz.at[at.l], dev))
    xz[at.l] = x1[at.l]
    yield
    arrived(copies)
    xp[at.pq] = xz[0] + xz[1] + xz[2] + xz[3]
    copies = []
    for k, dev in at.sum_plane():
        copies.append(links.start(xp.at[at.pq], xp.at[at.pq], dev))
    yield
    arrived(copies)
    total = xp[0]
    for k in range(1, 16):
        total = total + xp[k]
    place = xo.at[mine, rows(at.l * 128, 128)]
    place[...] = total
    copies = []
    for lt, dev in at.sum_line():
        copies.append(links.start(place, place, dev))
    yield
    arrived(copies)
    last = links.start(xo.at[mine], xo.at[mine], at.sibling)
    yield
    arrived([last])


def step(generator):
    for _ in generator:
        return True
    return False


def finish(generator):
    while step(generator):
        pass


def head(h, part=0):
    return pl.ds(part * D + h * HS, HS)


def block(b):
    return pl.ds(b * RB, RB)


def lower(b):
    row = lax.broadcasted_iota(jnp.int32, (RB, (b + 1) * RB), 0) + b * RB
    col = lax.broadcasted_iota(jnp.int32, (RB, (b + 1) * RB), 1)
    return col <= row


def kernel(
    parents, counts_in, occupancy_in, sib_in, gain_in, w_qkv_in, w_out_in, w_head_in,
    e_full, l_full, small_out,
    window, ends, offz, offp, offs, inputs, inv_in, normed, packed, onehot,
    scores, numer, resid, inv_out, final, attended, d_logits, d_resid, d_resid_b, wide, grads, d_packed,
    d_local, states, prefix, qstates, suffix,
    f_sib, f_chip, f_z, f_p, f_ret, f_e, f_give,
    b_sib, b_chip, b_z, b_p, b_ret, b_e, b_give,
    early, e_r0, e_own, e_r1, e_z, e_r2, e_p, e_ag, e_pa,
    late, l_r0, l_own, l_r1, l_z, l_r2, l_p, l_ag, l_pa,
    small, x0, x1, xz, xp,
    counts, occupancy, sib_table, gain, w_qkv, w_out, w_head, pair_rows, pair_kv, moved,
    send, recv, load,
):
    at = Place()
    links = Links(send, recv)
    own = pl.ds(PAR, PAR)
    pairs = [
        (counts_in, counts), (parents, window.at[own]), (sib_in, sib_table), (gain_in, gain), (w_qkv_in, w_qkv),
        (occupancy_in, occupancy), (w_out_in, w_out), (w_head_in, w_head),
    ]
    loads = [pltpu.make_async_copy(src, dst, load.at[i]) for i, (src, dst) in enumerate(pairs)]
    for copy in loads:
        copy.start()
    all_here = greet(at)

    loads[0].wait()
    count = jnp.broadcast_to(counts[...].astype(F32), (16, PAR))
    whole = jnp.sum(count[:8], axis=1, keepdims=True)
    offs[0] = jnp.broadcast_to(whole, (8, 128))
    tri = (
        lax.broadcasted_iota(jnp.int32, (PAR, PAR), 0) <= lax.broadcasted_iota(jnp.int32, (PAR, PAR), 1)
    ).astype(BF16)
    local_ends = dot(count.astype(BF16), tri)[:8]
    ends[1, :8] = local_ends
    ends[1, 8:] = count[:8]
    count_col = count[:8].T[:, :1]
    start_col = (local_ends - count[:8]).T[:, :1]
    for copy in loads[1:4]:
        copy.wait()
    for r in range(8):
        value = (window[own, :].astype(F32) + sib_table[r : r + 1, :].astype(F32)).astype(BF16).astype(F32)
        inverse = lax.rsqrt(jnp.mean(value * value, axis=-1, keepdims=True) + 1e-06)
        inverse = jnp.where(count_col > float(r), inverse, 0.0)
        rows_r = (value * inverse * gain[...]).astype(BF16)
        if r == 0:
            for copy in loads[4:]:
                copy.wait()
        pair_kv[pl.ds(r * PAR, PAR), :] = dot(rows_r, w_qkv[:, pl.ds(D, 2 * D)]).astype(BF16)
    for h in range(HEADS):
        states[pl.ds(h * HS, HS), :] = dot_tn(pair_kv[:, head(h)], pair_kv[:, head(h, 1)])
    all_here()

    first = links.start(offs.at[0], offs.at[1], at.sibling)
    forward = scan(at, links, states, prefix, f_sib, f_chip, f_z, f_p, f_ret, f_e, f_give, False)
    step(forward)
    arrived([first])
    offset = jnp.where(at.c == 1, offs[1], 0.0)
    offz[at.z] = offs[0] + offs[1]
    copies = [links.start(offz.at[at.z], offz.at[at.z], dev) for zt, dev in at.line()]
    step(forward)
    halo = [
        links.start(ends.at[1], ends.at[0], at.next),
        links.start(ends.at[1], ends.at[2], at.prev),
        links.start(parents, window.at[pl.ds(0, PAR)], at.next),
        links.start(parents, window.at[pl.ds(2 * PAR, PAR)], at.prev),
    ]
    arrived(copies)
    offp[at.g] = offz[0] + offz[1] + offz[2] + offz[3]
    copies = [links.start(offp.at[at.g], offp.at[at.g], dev) for xt, yt, dev in at.plane()]
    for k in range(4):
        offset = offset + jnp.where(k < at.z, offz[k], 0.0)
    step(forward)
    arrived(copies)
    for k in range(16):
        offset = offset + jnp.where(k < at.g, offp[k], 0.0)
    shift = (at.me * N).astype(F32) - offset[:1, :1]
    arrived(halo)

    own_total = whole[:1, :1]
    low_total = ends[0, :1, PAR - 1 :]
    end_row = jnp.concatenate([ends[0, :1] - low_total, local_ends[:1], ends[2, :1] + own_total], axis=1)
    count_row = jnp.concatenate([ends[0, 8:9], count[:1], ends[2, 8:9]], axis=1)
    start_row = end_row - count_row
    lanes8 = lax.broadcasted_iota(jnp.int32, (128, 8), 0)
    spread = (lanes8 == lax.broadcasted_iota(jnp.int32, (128, 8), 1) + 16).astype(BF16)
    sib_rows = dot(spread, sib_table[...]).astype(BF16)
    lane = lax.broadcasted_iota(jnp.int32, (RB, 128), 1)
    for b in range(BLOCKS):
        place = lax.broadcasted_iota(jnp.int32, (RB, 1), 0).astype(F32) + (shift + float(b * RB))
        child = (start_row <= place) & (place < end_row)
        chosen = jnp.where(child, 1.0, 0.0).astype(BF16)
        start_of = jnp.sum(jnp.where(child, start_row, 0.0), axis=1, keepdims=True)
        rank = (place - start_of).astype(jnp.int32)
        hot = (rank + 16 == lane).astype(F32).astype(BF16)
        onehot[block(b), :] = hot
        value = (dot(chosen, window[...]) + dot(hot, sib_rows)).astype(BF16)
        inputs[block(b), :] = value
        value = value.astype(F32)
        inverse = lax.rsqrt(jnp.mean(value * value, axis=-1, keepdims=True) + 1e-06)
        inv_in[block(b), :] = inverse
        normed[block(b), :] = (value * inverse * gain[...]).astype(BF16)
    step(forward)
    packed[...] = dot(normed[...], w_qkv[...]).astype(BF16)

    for h in range(HEADS):
        for b in range(BLOCKS):
            keys, values = packed[: (b + 1) * RB, head(h, 1)], packed[: (b + 1) * RB, head(h, 2)]
            score = jnp.where(lower(b), dot_nt(packed[block(b), head(h)], keys), 0.0).astype(BF16)
            scores[h, block(b), : (b + 1) * RB] = score
            numer[block(b), head(h)] = dot(score, values)
        if h == 2:
            step(forward)
    for r in range(8):
        part = pl.ds(r * PAR, PAR)
        before = jnp.where(start_col + float(r) < shift, 1.0, 0.0)
        pair_rows[part, :] = (pair_kv[part, pl.ds(0, D)].astype(F32) * before).astype(BF16)
    place = lax.broadcasted_iota(jnp.int32, (N, 1), 0).astype(F32) + shift
    wide[...] = packed[:, pl.ds(D, D)].astype(F32) * jnp.where(place < 0.0, -1.0, 0.0)
    for h in range(HEADS):
        moved[pl.ds(h * HS, HS), :] = dot_tn(pair_rows[:, head(h)], pair_kv[:, head(h, 1)]) + dot_tn(
            wide[:, head(h)].astype(BF16), packed[:, head(h, 2)]
        )
    finish(forward)
    prefix[...] += moved[...]

    for h in range(HEADS):
        high, low = split(prefix[pl.ds(h * HS, HS), :])
        q = packed[:, head(h)]
        wide[:, head(h)] = dot(q, high) + dot(q, low)
    scale = float(DEVS * N) ** (-0.5)
    lane8 = lax.broadcasted_iota(jnp.int32, (RB, 8), 1)
    symbols = jnp.broadcast_to(occupancy[...].astype(F32), (8, N)).T.astype(jnp.int32)
    inv_heads = []
    for b in range(BLOCKS):
        for h in range(HEADS):
            value = numer[block(b), head(h)] + wide[block(b), head(h)]
            numer[block(b), head(h)] = value
            inverse = lax.rsqrt(jnp.mean(value * value, axis=-1, keepdims=True) + 1e-05)
            attended[block(b), head(h)] = (value * inverse).astype(BF16)
            inv_heads.append(inverse)
    wide[...] = dot(attended[...], w_out[...])
    for b in range(BLOCKS):
        value = inputs[block(b), :].astype(F32) + wide[block(b), :]
        resid[block(b), :] = value
        inverse = lax.rsqrt(jnp.mean(value * value, axis=-1, keepdims=True) + 1e-06)
        inv_out[block(b), :] = inverse
        last = (value * inverse).astype(BF16)
        final[block(b), :] = last
        logits = dot_nt(last, w_head[...])
        target = ((symbols[b * RB : (b + 1) * RB] >> lane8) & 1).astype(F32)
        small_grad = ((jax.nn.sigmoid(logits) - target) * scale).astype(BF16)
        d_logits[block(b), :] = small_grad
        d_final = dot(small_grad, w_head[...])
        mean = jnp.mean(d_final * value, axis=-1, keepdims=True)
        d_value = inverse * d_final - value * (inverse * inverse * inverse) * mean
        d_resid[block(b), :] = d_value
        d_resid_b[block(b), :] = d_value.astype(BF16)
    wide[...] = dot_nt(d_resid_b[...], w_out[...])
    for b in range(BLOCKS):
        for h in range(HEADS):
            piece, value, inverse = wide[block(b), head(h)], numer[block(b), head(h)], inv_heads[b * HEADS + h]
            mean = jnp.mean(piece * value, axis=-1, keepdims=True)
            grads[block(b), head(h)] = (inverse * piece - value * (inverse * inverse * inverse) * mean).astype(BF16)
    for h in range(HEADS):
        qstates[pl.ds(h * HS, HS), :] = dot_tn(packed[:, head(h)], grads[:, head(h)])

    backward = scan(at, links, qstates, suffix, b_sib, b_chip, b_z, b_p, b_ret, b_e, b_give, True)
    step(backward)
    early[:, pl.ds(0, D)] = dot_tn(attended[...], d_resid_b[...])
    step(backward)
    for h in range(HEADS):
        high, low = split(prefix[pl.ds(h * HS, HS), :])
        g = grads[:, head(h)]
        wide[:, head(h)] = dot_nt(g, high) + dot_nt(g, low)
    d_local[...] = jnp.zeros_like(d_local)
    for h in range(HEADS):
        for b in range(BLOCKS):
            upto = pl.ds(0, (b + 1) * RB)
            g, q = grads[block(b), head(h)], packed[block(b), head(h)]
            back = jnp.where(lower(b), dot_nt(g, packed[upto, head(h, 2)]), 0.0).astype(BF16)
            dq = dot(back, packed[upto, head(h, 1)]) + wide[block(b), head(h)]
            d_packed[block(b), head(h)] = dq.astype(BF16)
            d_local[upto, head(h)] += dot_tn(back, q)
            d_local[upto, head(h, 1)] += dot_tn(scores[h, block(b), upto], g)
        if h == 1:
            step(backward)
    step(backward)
    early[:, pl.ds(D, D)] = dot_tn(normed[...], d_packed[:, pl.ds(0, D)])
    early_sum = reduce_all(at, links, early, e_r0, e_own, e_r1, e_z, e_r2, e_p, e_ag, e_pa, e_full)
    step(early_sum)
    wide[...] = dot_nt(d_packed[:, pl.ds(0, D)], w_qkv[:, pl.ds(0, D)])
    step(backward)
    step(early_sum)
    finish(backward)

    for h in range(HEADS):
        high, low = split(suffix[pl.ds(h * HS, HS), :])
        k, v = packed[:, head(h, 1)], packed[:, head(h, 2)]
        d_packed[:, head(h, 1)] = (d_local[:, head(h)] + dot_nt(v, high) + dot_nt(v, low)).astype(BF16)
        d_packed[:, head(h, 2)] = (d_local[:, head(h, 1)] + dot(k, high) + dot(k, low)).astype(BF16)
    late[...] = dot_tn(normed[...], d_packed[:, pl.ds(D, 2 * D)])
    late_sum = reduce_all(at, links, late, l_r0, l_own, l_r1, l_z, l_r2, l_p, l_ag, l_pa, l_full)
    step(late_sum)
    step(late_sum)
    step(early_sum)
    wide[...] += dot_nt(d_packed[:, pl.ds(D, 2 * D)], w_qkv[:, pl.ds(D, 2 * D)])
    grad_gain = jnp.zeros((1, D), F32)
    grad_sib = jnp.zeros((128, D), F32)
    for b in range(BLOCKS):
        value, inverse, slope = inputs[block(b), :].astype(F32), inv_in[block(b), :], wide[block(b), :]
        grad_gain = grad_gain + jnp.sum(slope * value * inverse, axis=0, keepdims=True)
        scaled = slope * gain[...]
        mean = jnp.mean(scaled * value, axis=-1, keepdims=True)
        d_in = inverse * scaled - value * (inverse * inverse * inverse) * mean + d_resid[block(b), :]
        high, low = split(d_in)
        grad_sib = grad_sib + dot_tn(onehot[block(b), :], high) + dot_tn(onehot[block(b), :], low)
    small[pl.ds(0, 8), :] = dot_tn(d_logits[...], final[...])
    small[pl.ds(8, 8), :] = jnp.broadcast_to(grad_gain, (8, D))
    small[pl.ds(16, 16), :] = grad_sib[16:32]
    small_sum = reduce_small(at, links, small, small_out, x0, x1, xz, xp)
    step(small_sum)
    more = True
    while more:
        more = step(late_sum)
        step(small_sum)
        step(early_sum)
    finish(early_sum)
    finish(small_sum)
    links.finish()


def vm(shape, dtype=F32):
    return pltpu.VMEM(shape, dtype)


def scan_buffers():
    coded = [vm((k, 80, 128), jnp.int16) for k in (4, 4, 16, 4, 4)]
    return [vm((256, HS)), *coded, vm((256, HS))]


def sum_buffers():
    i16 = jnp.int16
    return [
        vm((N, 1024)), vm((4, 64, 1024)), vm((512, 128)), vm((3, 528, 128), i16), vm((3, 528, 128), i16),
        vm((16, 48, 128), i16), vm((15, 48, 128), i16), vm((48, 128), i16), vm((16, 48, 128), i16),
    ]


def shards(parent_rows, counts, occupancy, sib_table, gain, w_qkv, w_out, w_head):
    scratch = [
        vm((3 * PAR, D), BF16), vm((3, 16, PAR)), vm((4, 8, 128)), vm((16, 8, 128)), vm((2, 8, 128)),
        vm((N, D), BF16), vm((N, 1)), vm((N, D), BF16), vm((N, 3 * D), BF16), vm((N, 128), BF16),
        vm((HEADS, N, N), BF16), vm((N, D)), vm((N, D)), vm((N, 1)), vm((N, D), BF16), vm((N, D), BF16),
        vm((N, 8), BF16), vm((N, D)), vm((N, D), BF16), vm((N, D)), vm((N, D), BF16), vm((N, 3 * D), BF16),
        vm((N, 2 * D)), vm((N, HS)), vm((N, HS)), vm((N, HS)), vm((N, HS)),
        *scan_buffers(), *scan_buffers(), *sum_buffers(), *sum_buffers(),
        vm((32, D)), vm((16, D)), vm((4, 16, 128)), vm((4, 16, 128)), vm((16, 16, 128)),
        vm((1, PAR), jnp.int32), vm((1, N), jnp.int32), vm((8, D), BF16), vm((1, D)), vm((D, 3 * D), BF16), vm((D, D), BF16),
        vm((8, D), BF16), vm((8 * PAR, D), BF16), vm((8 * PAR, 2 * D), BF16), vm((N, HS)),
        pltpu.SemaphoreType.DMA((COPIES,)), pltpu.SemaphoreType.DMA((COPIES,)), pltpu.SemaphoreType.DMA((8,)),
    ]
    spec = pl.BlockSpec(memory_space=pltpu.VMEM)
    codes = jax.ShapeDtypeStruct((2, 4, 544, 128), jnp.int16)
    early, late, small = pl.pallas_call(
        kernel,
        out_shape=[codes, codes, jax.ShapeDtypeStruct((32, D), F32)],
        in_specs=[pl.BlockSpec(memory_space=pltpu.HBM)] * 8,
        out_specs=[spec] * 3,
        scratch_shapes=scratch,
        compiler_params=pltpu.CompilerParams(
            collective_id=0, has_side_effects=True, vmem_limit_bytes=58 * 1024 * 1024
        ),
        name="train_step",
    )(
        parent_rows, counts.reshape(1, PAR), occupancy.reshape(1, N), sib_table, gain.reshape(1, D),
        w_qkv, w_out, w_head.T,
    )
    hbm = pl.BlockSpec(memory_space=pl.ANY)
    shapes = [(D, 3 * D), (D, D), (8, D), (1, D), (8, D)]
    grad_qkv, grad_out, grad_head, grad_gain, grad_sib = pl.pallas_call(
        decode,
        in_specs=[hbm, hbm, spec],
        out_specs=[hbm, hbm, spec, spec, spec],
        out_shape=[jax.ShapeDtypeStruct(shape, F32) for shape in shapes],
        scratch_shapes=[
            vm((8, 544, 128), jnp.int16), vm((8, 544, 128), jnp.int16), vm((D, 3 * D)), vm((D, D)),
            pltpu.SemaphoreType.DMA((16,)), pltpu.SemaphoreType.DMA((16,)),
        ],
        compiler_params=pltpu.CompilerParams(vmem_limit_bytes=58 * 1024 * 1024),
        name="decode",
    )(early, late, small)
    return grad_qkv, grad_out, grad_head.T, grad_gain.reshape(D), grad_sib


def solution(mesh):
    placed = (P("seq", None), P("seq"), P("seq"), P(), P(), P(), P(), P())
    return jax.shard_map(
        shards, mesh=mesh, in_specs=placed, out_specs=(P(), P(), P(), P(), P()), check_vma=False
    )
```
